256 devices in a mesh: section: 16 (over z, y_lo), fsdp: 16 (over y_hi, x, core).
Axes of the slice: x: 4, y: 4 (y_hi: 2, y_lo: 2; y = y_hi * 2 + y_lo), z: 8, core: 2. Of those that a mesh axis runs over, the one named last changes fastest.
Arguments:
- inputs: bfloat16 [8, 512, 6144], P(None, 'fsdp'), may hold values from -6 to 6
- out_grad: bfloat16 [8, 512, 6144], P(None, 'fsdp'), may hold values from -0.119628906 to 0.119628906
- down_proj: bfloat16 [16, 6144, 128], P('section', 'fsdp'), may hold values from -0.078125 to 0.078125
- gain: bfloat16 [16, 6144], P('section', 'fsdp'), may hold values from 0.5 to 1.5
- up_proj: bfloat16 [16, 128, 6144], P('section', None, 'fsdp'), may hold values from -0.5 to 0.5
Outputs:
- grad_down: float32 [16, 6144, 128], P('section', 'fsdp')
- grad_gain: float32 [16, 6144], P('section', 'fsdp')
- grad_up: float32 [16, 128, 6144], P('section', None, 'fsdp')
The draws below stay inside these ranges and needn't reach their ends.
All inputs are finite; a program needn't handle non-finite values.
Results may differ from the reference program's by a relative error of at most 0.04.
Values may be sent and summed in bfloat16 or wider, within the bound.
No kernel may reach another device: no remote copies, remote signals or barrier semaphores. Data moves between devices by JAX's collectives and lax.ppermute only.
A program may use at most 64 MiB of HBM per device.

```python
import jax
import jax.numpy as jnp
from jax import lax

D = 6144
RANK = 128
MICRO = 8
MB_ROWS = 32
SECTIONS = 16
TOKENS = 512
N_FSDP = 16


def shard_levels(rng, extent, pieces, smallest, high):
    level, own = 1.0, jax.random.fold_in(rng, 6)
    for dim, shards_of in pieces:
        heights = jnp.exp(jax.random.uniform(jax.random.fold_in(own, dim), (shards_of,), jnp.float32, smallest / len(pieces), high / len(pieces)))
        level = level * jnp.repeat(heights, extent[dim] // shards_of).reshape([-1 if axis == dim else 1 for axis in range(len(extent))])
    return level


def noise(key, shape, deviation, most, shards=(), kind=jnp.bfloat16):
    drawn = jax.random.normal(key, shape, jnp.float32) * deviation
    if len(shards) > 0:
        drawn = shard_levels(key, shape, shards, -0.22, 0.18) * drawn
    return jnp.clip(drawn, min=-most, max=most).astype(kind)


def setup_inputs(seed: int = 0) -> dict:
    key_of = jax.random.split(jax.random.key(seed), 6)
    inputs = noise(key_of[0], (MICRO, TOKENS, D), 1.0, 6.0, ((1, 16),))
    out_grad = noise(key_of[1], (MICRO, TOKENS, D), 0.02, 0.119628906, ((1, 16),))
    down_proj = noise(key_of[2], (SECTIONS, D, RANK), D ** -0.5, 0.078125, ((0, 16), (1, 16)))
    gain = jnp.clip(1.0 + 0.1 * jax.random.normal(key_of[3], (SECTIONS, D), jnp.float32), 0.5, 1.5).astype(jnp.bfloat16)
    up_proj = noise(key_of[4], (SECTIONS, RANK, D), RANK ** -0.5, 0.5, ((0, 16), (2, 16)))
    return {"inputs": inputs, "out_grad": out_grad, "down_proj": down_proj, "gain": gain, "up_proj": up_proj}


def forward_layer(hidden, gain_row, down, up):
    wide = hidden.astype(jnp.float32)
    inverse = lax.rsqrt(lax.optimization_barrier(jnp.mean(wide * wide, axis=-1, keepdims=True)) + 1e-05)
    normed = (wide * inverse * gain_row.astype(jnp.float32)).astype(jnp.bfloat16)
    act = jnp.dot(normed, down, preferred_element_type=jnp.float32)
    squashed = jax.nn.silu(act).astype(jnp.bfloat16)
    return (wide + jnp.dot(squashed, up, preferred_element_type=jnp.float32)).astype(jnp.bfloat16)

def recompute(hidden, gain_row, down):
    wide = hidden.astype(jnp.float32)
    inverse = lax.rsqrt(lax.optimization_barrier(jnp.mean(wide * wide, axis=-1, keepdims=True)) + 1e-05)
    unit = wide * inverse
    normed = (unit * gain_row.astype(jnp.float32)).astype(jnp.bfloat16)
    act = jnp.dot(normed, down, preferred_element_type=jnp.float32)
    return (inverse, unit, normed, act)

def backward_layer(hidden, upstream, gain_row, down, up):
    inverse, unit, normed, act = recompute(hidden, gain_row, down)
    lifted = lax.dot_general(upstream, up, (((1,), (1,)), ((), ())), preferred_element_type=jnp.float32)
    sigma = jax.nn.sigmoid(act)
    act_grad = (lifted * sigma * (1.0 + act * (1.0 - sigma))).astype(jnp.bfloat16)
    norm_grad = lax.dot_general(act_grad, down, (((1,), (1,)), ((), ())), preferred_element_type=jnp.float32)
    scaled = norm_grad * gain_row.astype(jnp.float32)
    centred = scaled - unit * lax.optimization_barrier(jnp.mean(scaled * unit, axis=-1, keepdims=True))
    grad_in = (upstream.astype(jnp.float32) + inverse * centred).astype(jnp.bfloat16)
    return (grad_in, act_grad, norm_grad * unit)

def reference(inputs, out_grad, down_proj, gain, up_proj):
    sections = down_proj.shape[0]
    batches = inputs.shape[0]
    width = inputs.shape[2]
    saved = [[None] * batches for _ in range(sections)]
    for micro in range(batches):
        hidden = inputs[micro]
        for level in range(sections):
            saved[level][micro] = hidden
            hidden = forward_layer(hidden, gain[level], down_proj[level], up_proj[level])
    upstreams = [[None] * batches for _ in range(sections)]
    slopes = [[None] * batches for _ in range(sections)]
    gain_terms = [[None] * batches for _ in range(sections)]
    for micro in range(batches):
        upstream = out_grad[micro]
        for level in range(sections - 1, -1, -1):
            upstreams[level][micro] = upstream
            upstream, act_grad, term = backward_layer(saved[level][micro], upstream, gain[level], down_proj[level], up_proj[level])
            slopes[level][micro] = act_grad
            gain_terms[level][micro] = term
    grads_down = []
    grads_gain = []
    grads_up = []
    for level in range(sections):
        hidden = jnp.stack(saved[level]).reshape(batches, N_FSDP, MB_ROWS, width)
        hidden = jnp.transpose(hidden, (1, 0, 2, 3)).reshape(N_FSDP * batches * MB_ROWS, width)
        carried = jnp.stack(upstreams[level]).reshape(batches, N_FSDP, MB_ROWS, width)
        carried = jnp.transpose(carried, (1, 0, 2, 3)).reshape(N_FSDP, batches * MB_ROWS, width)
        slope = jnp.stack(slopes[level]).reshape(batches, N_FSDP, MB_ROWS, -1)
        slope = jnp.transpose(slope, (1, 0, 2, 3)).reshape(N_FSDP, batches * MB_ROWS, -1)
        term = jnp.stack(gain_terms[level]).reshape(batches, N_FSDP, MB_ROWS, width)
        inverse, unit, normed, act = recompute(hidden, gain[level], down_proj[level])
        squashed = jax.nn.silu(act).astype(jnp.bfloat16).reshape(N_FSDP, batches * MB_ROWS, -1)
        normed = normed.reshape(N_FSDP, batches * MB_ROWS, width)
        part_down = jnp.einsum('gtd,gtr->gdr', normed.astype(jnp.float32), slope.astype(jnp.float32))
        part_up = jnp.einsum('gtr,gtd->grd', squashed.astype(jnp.float32), carried.astype(jnp.float32))
        part_gain = lax.optimization_barrier(jnp.sum(term, axis=(0, 2)))
        grads_down.append(lax.optimization_barrier(jnp.sum(part_down.astype(jnp.bfloat16).astype(jnp.float32), axis=0)))
        grads_up.append(lax.optimization_barrier(jnp.sum(part_up.astype(jnp.bfloat16).astype(jnp.float32), axis=0)))
        grads_gain.append(lax.optimization_barrier(jnp.sum(part_gain.astype(jnp.bfloat16).astype(jnp.float32), axis=0)))
    return (jnp.stack(grads_down), jnp.stack(grads_gain), jnp.stack(grads_up))
```

```python
import functools

import jax
import jax.numpy as jnp
from jax import lax
from jax.experimental import pallas as pl
from jax.experimental.pallas import tpu as pltpu
from jax.sharding import PartitionSpec as P

F32 = jnp.float32
BF16 = jnp.bfloat16


def dot(a, b, dims):
    return lax.dot_general(a, b, (dims, ((), ())), preferred_element_type=F32)


NN = ((1,), (0,))
NT = ((1,), (1,))
TN = ((0,), (0,))


def hop(block, axis, stride, count, offset):
    route = []
    for i in range(lax.axis_size(axis)):
        place = (i // stride) % count
        route.append((i, i + ((place + offset) % count - place) * stride))
    return lax.ppermute(block, axis, route)


def gather_fsdp(shard):
    me = lax.axis_index("fsdp")
    y, x, core = me // 8, (me // 2) % 4, me % 2
    both = jnp.zeros((2, 4, 2) + shard.shape, shard.dtype)
    other = hop(shard, "fsdp", 8, 2, 1)
    first = jnp.where(y == 0, shard, other)
    second = jnp.where(y == 0, other, shard)
    pair = jnp.stack([first, second])
    half = pair.shape[1] // 2
    from_left = hop(pair, "fsdp", 2, 4, 1)
    from_right = hop(pair, "fsdp", 2, 4, -1)
    far_a = hop(from_left[:, :half], "fsdp", 2, 4, 1)
    far_b = hop(from_right[:, half:], "fsdp", 2, 4, -1)
    far = jnp.concatenate([far_a, far_b], axis=1)
    row = jnp.zeros((2, 4) + shard.shape, shard.dtype)
    for k, piece in enumerate((pair, from_left, far, from_right)):
        row = lax.dynamic_update_slice(row, piece[:, None], (0, (x - k) % 4, 0, 0))
    mate = hop(row, "fsdp", 1, 2, 1)
    both = lax.dynamic_update_slice(both, row[:, :, None], (0, 0, core, 0, 0))
    both = lax.dynamic_update_slice(both, mate[:, :, None], (0, 0, 1 - core, 0, 0))
    return both.reshape((16,) + shard.shape)


def gather_section(block):
    return lax.all_to_all(
        jnp.broadcast_to(block[None], (16,) + block.shape), "section", 0, 0, tiled=True
    )


def gather_rest(slab):
    return jnp.swapaxes(gather_fsdp(slab.reshape(-1, slab.shape[-1])).reshape((16,) + slab.shape), 0, 1)


def chain(width, a_ref, norm_ref, z_ref, q_ref, p_ref, c_ref):
    layers = a_ref.shape[0]
    rank = z_ref.shape[2]
    cut = [slice(rank * i, rank * (i + 1)) for i in range(layers)]
    a_of = lambda s, part: a_ref[s, :, cut[part]].astype(F32)
    scale = 1.0 / width
    total = norm_ref[...]
    w = [a_of(s, 1) for s in range(layers)]
    q, slope, act_of, inverse_of = [], [], [], []
    for s in range(layers):
        inverse = lax.rsqrt(jnp.maximum(total, 0.0) * scale + 1e-05)
        raw = a_of(s, 0)
        if s > 1:
            raw = raw + dot(jnp.concatenate(q[: s - 1], axis=1), z_ref[s, : rank * (s - 1), :], NN)
        if s > 0:
            raw = raw + dot(q[s - 1], z_ref[s, cut[s - 1], :], NN)
        act = raw * inverse
        sigma = jax.nn.sigmoid(act)
        now = (act * sigma).astype(BF16)
        wide = now.astype(F32)
        own = dot(now, z_ref[s, cut[s], :], NT)
        total = total + jnp.sum(wide * (2.0 * w[s] + own), axis=1, keepdims=True)
        w[s] = w[s] + own
        if s + 1 < layers:
            ahead = dot(now, z_ref[s, rank * (s + 1) :, :], NT)
            for k in range(s + 1, layers):
                w[k] = w[k] + ahead[:, cut[k - s - 1]]
        q.append(now)
        q_ref[:, cut[s]] = now
        slope.append(sigma * (1.0 + act * (1.0 - sigma)))
        act_of.append(act)
        inverse_of.append(inverse)
    lift = [a_of(s, 2) for s in range(layers)]
    shrink = jnp.zeros_like(norm_ref)
    scaled = [None] * layers
    lane = lax.broadcasted_iota(jnp.int32, c_ref.shape, 1)
    kept = jnp.zeros(c_ref.shape, F32)
    for s in range(layers - 1, -1, -1):
        up = lift[s]
        if s + 1 < layers:
            up = up - shrink * w[s]
            up = up - dot(scaled[s + 1], z_ref[s, cut[s + 1], :], NN)
        if s + 2 < layers:
            up = up - dot(
                jnp.concatenate(scaled[s + 2 :], axis=1), z_ref[s, rank * (s + 2) :, :], NN
            )
        grad = (up * slope[s]).astype(BF16).astype(F32)
        now = (grad * inverse_of[s]).astype(BF16)
        p_ref[:, cut[s]] = now
        kept = jnp.where(lane == s, shrink, kept)
        scaled[s] = (shrink * q[s].astype(F32)).astype(BF16)
        if s > 0:
            back = dot(now, z_ref[s, : rank * s, :], NT)
            for k in range(s):
                lift[k] = lift[k] + back[:, cut[k]]
        mean = jnp.sum(grad * act_of[s], axis=1, keepdims=True) * scale
        shrink = shrink + inverse_of[s] * inverse_of[s] * mean
    c_ref[...] = kept


def on_device(inputs, out_grad, down_proj, gain, up_proj):
    sections, groups = lax.axis_size("section"), lax.axis_size("fsdp")
    s = lax.axis_index("section")
    width = inputs.shape[2]
    x = inputs.reshape(-1, width)
    y = out_grad.reshape(-1, width)
    tokens = x.shape[0]
    few = tokens // sections
    down, gain_row, up = down_proj[0], gain[0].astype(F32), up_proj[0]
    piece, rank = down.shape

    scaled_down = (down.astype(F32) * gain_row[:, None]).astype(BF16)
    weights = jnp.concatenate([scaled_down, up.T], axis=1)
    up_all = lax.all_gather(up, "section", axis=0)
    down_all = lax.all_gather(scaled_down, "section", axis=0)

    whole = gather_fsdp(weights).reshape(width, 2 * rank)
    from_x = dot(x, whole, NN)
    from_y = dot(y, whole[:, rank:], NN)
    projected = jnp.concatenate([from_x, from_y], axis=1).astype(BF16)
    projected = lax.all_to_all(
        projected.reshape(sections, few, 3 * rank), "section", 0, 0, tiled=True
    )
    mine = lax.dynamic_slice_in_dim(x, s * few, few, 0).astype(F32)
    norm = jnp.sum(mine * mine, axis=1, keepdims=True)

    pairs = dot(up_all.reshape(sections * rank, piece), weights, NN)
    layer = lax.broadcasted_iota(jnp.int32, (sections * rank, 1), 0) // rank
    chosen = jnp.where(layer < s, pairs[:, :rank], pairs[:, rank:]).astype(BF16)
    chosen = lax.all_to_all(chosen.reshape(groups, rank, rank), "fsdp", 0, 0, tiled=True)
    block = jnp.sum(chosen.astype(F32), axis=0).astype(BF16)
    table = gather_rest(gather_section(block))
    table = table.reshape(sections, groups * rank, rank)

    q, p, c = pl.pallas_call(
        functools.partial(chain, width),
        out_shape=(
            jax.ShapeDtypeStruct((few, sections * rank), BF16),
            jax.ShapeDtypeStruct((few, sections * rank), BF16),
            jax.ShapeDtypeStruct((few, rank), F32),
        ),
        compiler_params=pltpu.CompilerParams(vmem_limit_bytes=40 * 2**20),
        name="chain",
    )(projected, norm, table)

    high = c.astype(BF16)
    low = (c - high.astype(F32)).astype(BF16)
    packed = jnp.concatenate([q, p, high, low], axis=1)
    packed = gather_section(packed).reshape(tokens, -1)
    span = sections * rank
    q_all, p_all = packed[:, :span], packed[:, span : 2 * span]
    c_all = packed[:, 2 * span : 2 * span + sections].astype(F32)
    c_all = c_all + packed[:, 2 * span + rank : 2 * span + rank + sections].astype(F32)
    q_s = lax.dynamic_slice_in_dim(q_all, s * rank, rank, 1)
    p_s = lax.dynamic_slice_in_dim(p_all, s * rank, rank, 1)
    c_s = lax.dynamic_slice_in_dim(c_all, s, 1, 1)
    cq_s = (c_s * q_s.astype(F32)).astype(BF16)
    cq_all = (
        jnp.repeat(c_all, rank, axis=1, total_repeat_length=span) * q_all.astype(F32)
    ).astype(BF16)

    left = dot(q_all, jnp.concatenate([p_s, cq_s], axis=1), TN)
    right_p = dot(p_all, q_s, TN)
    right_c = dot(cq_all, q_s, TN)
    first = jnp.where(layer < s, left[:, :rank], jnp.where(layer > s, right_p, 0.0))
    second = jnp.where(layer < s, left[:, rank:], right_c)
    cross = jnp.concatenate([first, second], axis=1).astype(BF16)
    cross = lax.all_to_all(cross.reshape(groups, rank, 2 * rank), "fsdp", 0, 0, tiled=True)
    cross = jnp.sum(cross.astype(F32), axis=0).astype(BF16)
    cross = gather_fsdp(cross).reshape(span, 2 * rank)

    part_x = dot(x, jnp.concatenate([p_s, -cq_s], axis=1), TN)
    part_y = dot(y, q_s, TN)
    part = jnp.concatenate([part_x[:, :rank], part_x[:, rank:] + part_y], axis=1).astype(BF16)
    part = lax.all_to_all(part.reshape(groups, piece, 2 * rank), "fsdp", 0, 0, tiled=True)
    part = jnp.sum(part.astype(F32), axis=0)

    zero = jnp.zeros((), BF16)
    before = jnp.where(layer < s, cross[:, :rank], zero)
    after = jnp.where(layer > s, cross[:, :rank], zero)
    by_up = dot(
        up_all.reshape(span, piece), jnp.concatenate([before, -cross[:, rank:]], axis=1), TN
    )
    by_down = lax.dot_general(
        down_all,
        after.reshape(sections, rank, rank),
        (((2,), (1,)), ((0,), (0,))),
        preferred_element_type=F32,
    ).sum(axis=0)
    held = part[:, :rank] + by_up[:, :rank]
    grad_up = (part[:, rank:] + by_up[:, rank:] + by_down).T
    grad_down = gain_row[:, None] * held
    grad_gain = jnp.sum(down.astype(F32) * held, axis=1)
    return (grad_down[None], grad_gain[None], grad_up[None])


def solution(mesh):
    placed = (
        P(None, "fsdp", None),
        P(None, "fsdp", None),
        P("section", "fsdp", None),
        P("section", "fsdp"),
        P("section", None, "fsdp"),
    )
    return jax.shard_map(
        on_device,
        mesh=mesh,
        in_specs=placed,
        out_specs=(P("section", "fsdp", None), P("section", "fsdp"), P("section", None, "fsdp")),
        check_vma=False,
    )
```

```python
import functools

import jax
import jax.numpy as jnp
from jax import lax
from jax.experimental import pallas as pl
from jax.experimental.pallas import tpu as pltpu
from jax.sharding import PartitionSpec as P

F32 = jnp.float32
BF16 = jnp.bfloat16
NN = ((1,), (0,))
NT = ((1,), (1,))
TN = ((0,), (0,))
MIB = 2**20
LENGTHS = (2, 2, 2, 1, 1)
STARTS = (0, 2, 4, 6, 7)


def dot(a, b, dims):
    return lax.dot_general(a, b, (dims, ((), ())), preferred_element_type=F32)


def hop(block, axis, stride, count, offset):
    route = []
    for i in range(lax.axis_size(axis)):
        place = (i // stride) % count
        route.append((i, i + ((place + offset) % count - place) * stride))
    return lax.ppermute(block, axis, route)


def across(block):
    route = []
    for section in range(16):
        for group in range(16):
            to = (section ^ 1) * 16 + (group ^ 8)
            route.append((section * 16 + group, to))
    return lax.ppermute(block, ("section", "fsdp"), route)


def gather_pieces(shard, same_along_section=False):
    other = across(shard) if same_along_section else hop(shard, "fsdp", 8, 2, 1)
    pair = jnp.concatenate([shard[None], other[None]])
    left = hop(pair, "fsdp", 2, 4, 1)
    right = hop(pair, "fsdp", 2, 4, -1)
    far_a = hop(left[:1], "fsdp", 2, 4, 1)
    far_b = hop(right[1:], "fsdp", 2, 4, -1)
    near = [pair, left, right, far_a, far_b]
    return near + [hop(piece, "fsdp", 1, 2, 1) for piece in near]


def places():
    me = lax.axis_index("fsdp")
    y, x, core = me // 8, (me // 2) % 4, me % 2
    steps = ((0, 0), (1, 0), (0, 3), (1, 3), (0, 1), (1, 1), (0, 2), (1, 2))
    found = []
    for c in (core, 1 - core):
        for i, o in steps:
            found.append(jnp.where(i == 0, y, 1 - y) * 8 + ((x + o) % 4) * 2 + c)
    return jnp.stack(found).astype(jnp.int32)


def gather_section(block):
    return lax.all_to_all(
        jnp.broadcast_to(block[None], (16,) + block.shape), "section", 0, 0, tiled=True
    )


def fold(keep, send, after=None):
    got = hop(send, "fsdp", 1, 2, 1)
    summed = (keep.astype(F32) + got.astype(F32)).astype(BF16)
    if after is not None:
        summed, _ = lax.optimization_barrier((summed, after))
    chips = [list(range(core, 16, 2)) for core in range(2)]
    return lax.all_to_all(summed, "fsdp", 0, 0, tiled=True, axis_index_groups=chips)


def each_piece(pieces):
    for c in range(2):
        for k, (length, start) in enumerate(zip(LENGTHS, STARTS)):
            for i in range(length):
                yield c * 8 + start + i, pieces[5 * c + k], i


def project(place_ref, x_ref, y_ref, *rest):
    pieces, out_ref = rest[:10], rest[10]
    size = pieces[0].shape[1]
    rank = pieces[0].shape[2] // 2
    from_x, from_y = 0.0, 0.0
    for at, piece, i in each_piece(pieces):
        span = pl.ds(pl.multiple_of(place_ref[at] * size, 128), size)
        from_x = from_x + dot(x_ref[:, span], piece[i], NN)
        from_y = from_y + dot(y_ref[:, span], piece[i, :, rank:], NN)
    out_ref[:, : 2 * rank] = from_x.astype(BF16)
    out_ref[:, 2 * rank :] = from_y.astype(BF16)


def chain(width, s_ref, place_ref, a_ref, norm_ref, *rest):
    pieces = rest[:10]
    pick_ref, keep_ref, send_ref = rest[10:13]
    z_ref, w_ref, lift_ref, act_ref, slope_ref, inv_ref = rest[13:19]
    q_ref, p_ref, sq_ref, sums_ref, sem = rest[19:]
    layers = a_ref.shape[0]
    rank = z_ref.shape[2]
    cut = [slice(rank * i, rank * (i + 1)) for i in range(layers)]
    copies = []
    for at, piece, i in each_piece(pieces):
        span = pl.ds(pl.multiple_of(place_ref[at] * rank, rank), rank)
        copies.append(pltpu.make_async_copy(piece.at[i], z_ref.at[:, span, :], sem.at[at]))
    for copy in copies:
        copy.start()
    for s in range(layers):
        w_ref[s] = a_ref[s, :, cut[1]].astype(F32)
        lift_ref[s] = a_ref[s, :, cut[2]].astype(F32)
    for copy in copies:
        copy.wait()
    scale = 1.0 / width
    total = norm_ref[...]
    for s in range(layers):
        inverse = lax.rsqrt(jnp.maximum(total, 0.0) * scale + 1e-05)
        raw = a_ref[s, :, cut[0]].astype(F32)
        if s > 0:
            raw = raw + dot(q_ref[:, : rank * s], z_ref[s, : rank * s, :], NN)
        act = raw * inverse
        sigma = jax.nn.sigmoid(act)
        now = (act * sigma).astype(BF16)
        q_ref[:, cut[s]] = now
        slope_ref[s] = sigma * (1.0 + act * (1.0 - sigma))
        act_ref[s] = act
        inv_ref[s] = jnp.broadcast_to(inverse, act.shape)
        wide = now.astype(F32)
        own = dot(now, z_ref[s, cut[s], :], NT)
        here = w_ref[s]
        total = total + jnp.sum(wide * (2.0 * here + own), axis=1, keepdims=True)
        w_ref[s] = here + own
        if s + 1 < layers:
            ahead = dot(now, z_ref[s, rank * (s + 1) :, :], NT)
            for k in range(s + 1, layers):
                w_ref[k] += ahead[:, cut[k - s - 1]]
    shrink = jnp.zeros_like(total)
    for s in range(layers - 1, -1, -1):
        up = lift_ref[s]
        if s + 1 < layers:
            up = up - shrink * w_ref[s]
            up = up - dot(sq_ref[:, rank * (s + 1) :], z_ref[s, rank * (s + 1) :, :], NN)
        grad = (up * slope_ref[s]).astype(BF16).astype(F32)
        inverse = inv_ref[s]
        now = (grad * inverse).astype(BF16)
        p_ref[:, cut[s]] = now
        sq_ref[:, cut[s]] = (shrink * q_ref[:, cut[s]].astype(F32)).astype(BF16)
        if s > 0:
            back = dot(now, z_ref[s, : rank * s, :], NT)
            for k in range(s):
                lift_ref[k] += back[:, cut[k]]
        mean = jnp.sum(grad * act_ref[s] * inverse * inverse, axis=1, keepdims=True) * scale
        shrink = shrink + mean
    here = pl.ds(pl.multiple_of(s_ref[0] * rank, rank), rank)
    p_t, q_t, sq_t = p_ref[:, here].T, q_ref[:, here].T, sq_ref[:, here].T
    both = jnp.concatenate([p_t, -sq_t], axis=0)
    pick_ref[: 2 * rank] = both
    pick_ref[2 * rank :] = q_t
    for j in range(layers):

        @pl.when(j < s_ref[0])
        def _():
            sums_ref[...] = dot(both, q_ref[:, cut[j]], NN).astype(BF16)

        @pl.when(j >= s_ref[0])
        def _():
            first = dot(q_t, p_ref[:, cut[j]], NN)
            first = jnp.where(j == s_ref[0], 0.0, first)
            sums_ref[:rank] = first.astype(BF16)
            sums_ref[rank:] = (-dot(q_t, sq_ref[:, cut[j]], NN)).astype(BF16)

        @pl.when(s_ref[1] == j % 2)
        def _():
            keep_ref[j // 2] = sums_ref[...]

        @pl.when(s_ref[1] != j % 2)
        def _():
            send_ref[j // 2] = sums_ref[...]


def outer(s_ref, pick_ref, x_ref, y_ref, keep_ref, send_ref):
    rank = pick_ref.shape[0] // 3
    piece = keep_ref.shape[2]
    from_x = dot(pick_ref[: 2 * rank], x_ref[...], NN)
    from_y = dot(pick_ref[2 * rank :], y_ref[...], NN)
    both = jnp.concatenate([from_x[:rank], from_x[rank:] + from_y], axis=0).astype(BF16)
    even, odd = both[:, :piece], both[:, piece:]
    first = s_ref[1] == 0
    keep_ref[0] = jnp.where(first, even, odd)
    send_ref[0] = jnp.where(first, odd, even)


def finish(s_ref, place_ref, part_ref, up_ref, down_ref, own_ref, gain_ref, *rest):
    pieces = rest[:10]
    down_out, gain_out, up_out, cross_ref, sem = rest[10:]
    layers, rank, piece = up_ref.shape
    copies = []
    for at, array, i in each_piece(pieces):
        span = pl.ds(pl.multiple_of(place_ref[at] * rank, rank), rank)
        copies.append(pltpu.make_async_copy(array.at[i], cross_ref.at[:, span], sem.at[at]))
    for copy in copies:
        copy.start()
    held = part_ref[0].astype(F32)
    for k in range(1, part_ref.shape[0]):
        held = held + part_ref[k].astype(F32)
    for copy in copies:
        copy.wait()
    span = layers * rank
    lane = lax.broadcasted_iota(jnp.int32, (2 * rank, span), 1)
    row = lax.broadcasted_iota(jnp.int32, (2 * rank, span), 0)
    split = s_ref[0] * rank
    cross = cross_ref[...]
    zero = jnp.zeros_like(cross)
    with_up = jnp.where(jnp.logical_or(row >= rank, lane < split), cross, zero)
    after = jnp.where(lane[:rank] >= split + rank, cross[:rank], zero[:rank])
    held = held + dot(with_up, up_ref[...].reshape(span, piece), NN)
    held_up = held[rank:]
    for k in range(layers):
        held_up = held_up + dot(after[:, rank * k : rank * (k + 1)], down_ref[k], NT)
    up_out[...] = held_up
    held_down = held[:rank]
    down_out[...] = (held_down * gain_ref[...]).T
    gain_out[...] = jnp.sum(own_ref[...].astype(F32).T * held_down, axis=0, keepdims=True)


def on_device(inputs, out_grad, down_proj, gain, up_proj):
    sections, groups = lax.axis_size("section"), lax.axis_size("fsdp")
    s = lax.axis_index("section")
    here = jnp.stack([s, lax.axis_index("fsdp") % 2]).astype(jnp.int32)
    place = places()
    width = inputs.shape[2]
    x = inputs.reshape(-1, width)
    y = out_grad.reshape(-1, width)
    tokens = x.shape[0]
    down, gain_row, up = down_proj[0], gain[0].astype(F32), up_proj[0]
    piece, rank = down.shape
    smem = pl.BlockSpec(memory_space=pltpu.SMEM)
    vmem = pl.BlockSpec(memory_space=pltpu.VMEM)
    anywhere = pl.BlockSpec(memory_space=pl.ANY)

    scaled_down = (down.astype(F32) * gain_row[:, None]).astype(BF16)
    weights = jnp.concatenate([scaled_down, up.T], axis=1)
    up_all = gather_section(up)

    projected = pl.pallas_call(
        project,
        out_shape=jax.ShapeDtypeStruct((tokens, 3 * rank), BF16),
        in_specs=[smem] + [vmem] * 12,
        out_specs=vmem,
        compiler_params=pltpu.CompilerParams(vmem_limit_bytes=32 * MIB),
        name="project",
    )(place, x, y, *gather_pieces(weights))
    projected = lax.all_gather(projected, "section", axis=0)
    norm = jnp.sum(jnp.square(x.astype(F32)), axis=1, keepdims=True)

    pairs = dot(up_all.reshape(sections * rank, piece), weights, NN)
    layer = lax.broadcasted_iota(jnp.int32, (sections * rank, 1), 0) // rank
    chosen = jnp.where(layer < s, pairs[:, :rank], pairs[:, rank:]).astype(BF16)
    chosen = lax.all_to_all(chosen.reshape(groups, rank, rank), "fsdp", 0, 0, tiled=True)
    block = jnp.sum(chosen.astype(F32), axis=0).astype(BF16)
    table = gather_pieces(gather_section(block), same_along_section=True)

    big = lambda kind: pltpu.VMEM((sections, tokens, rank), kind)
    flat = pltpu.VMEM((tokens, sections * rank), BF16)
    half = groups // 2
    pick, cross, cross_out = pl.pallas_call(
        functools.partial(chain, width),
        out_shape=(
            jax.ShapeDtypeStruct((3 * rank, tokens), BF16),
            jax.ShapeDtypeStruct((half, 2 * rank, rank), BF16),
            jax.ShapeDtypeStruct((half, 2 * rank, rank), BF16),
        ),
        in_specs=[smem, smem, vmem, vmem] + [anywhere] * 10,
        out_specs=(vmem,) * 3,
        scratch_shapes=[pltpu.VMEM((sections, sections * rank, rank), BF16)]
        + [big(F32)] * 5
        + [flat] * 3
        + [pltpu.VMEM((2 * rank, rank), BF16), pltpu.SemaphoreType.DMA((16,))],
        compiler_params=pltpu.CompilerParams(vmem_limit_bytes=44 * MIB),
        name="chain",
    )(here, place, projected, norm, *table)
    late, _ = lax.optimization_barrier((scaled_down, projected))
    down_all = lax.all_gather(late, "section", axis=0)

    cross = fold(cross, cross_out)
    cross = jnp.sum(cross.astype(F32), axis=0).astype(BF16)
    cross = gather_pieces(cross)

    part, part_out = pl.pallas_call(
        outer,
        grid=(half,),
        out_shape=(jax.ShapeDtypeStruct((half, 2 * rank, piece), BF16),) * 2,
        in_specs=[
            smem,
            pl.BlockSpec((3 * rank, tokens), lambda i: (0, 0)),
            pl.BlockSpec((tokens, 2 * piece), lambda i: (0, i)),
            pl.BlockSpec((tokens, 2 * piece), lambda i: (0, i)),
        ],
        out_specs=(pl.BlockSpec((1, 2 * rank, piece), lambda i: (i, 0, 0)),) * 2,
        name="outer",
    )(here, pick, x, y)
    part = fold(part, part_out, cross[1])

    grad_down, grad_gain, grad_up = pl.pallas_call(
        finish,
        out_shape=(
            jax.ShapeDtypeStruct((piece, rank), F32),
            jax.ShapeDtypeStruct((1, piece), F32),
            jax.ShapeDtypeStruct((rank, piece), F32),
        ),
        in_specs=[smem, smem] + [vmem] * 5 + [anywhere] * 10,
        out_specs=(vmem,) * 3,
        scratch_shapes=[
            pltpu.VMEM((2 * rank, groups * rank), BF16),
            pltpu.SemaphoreType.DMA((16,)),
        ],
        compiler_params=pltpu.CompilerParams(vmem_limit_bytes=32 * MIB),
        name="finish",
    )(here, place, part, up_all, down_all, down, gain_row[None], *cross)
    return (grad_down[None], grad_gain, grad_up[None])


def solution(mesh):
    placed = (
        P(None, "fsdp", None),
        P(None, "fsdp", None),
        P("section", "fsdp", None),
        P("section", "fsdp"),
        P("section", None, "fsdp"),
    )
    return jax.shard_map(
        on_device,
        mesh=mesh,
        in_specs=placed,
        out_specs=(P("section", "fsdp", None), P("section", "fsdp"), P("section", None, "fsdp")),
        check_vma=False,
    )
```

```python
import functools

import jax
import jax.numpy as jnp
from jax import lax
from jax.experimental import pallas as pl
from jax.experimental.pallas import tpu as pltpu
from jax.sharding import PartitionSpec as P

F32 = jnp.float32
BF16 = jnp.bfloat16
NN = ((1,), (0,))
NT = ((1,), (1,))
TN = ((0,), (0,))
MIB = 2**20


def dot(a, b, dims):
    return lax.dot_general(a, b, (dims, ((), ())), preferred_element_type=F32)


def hop(block, axis, stride, count, offset):
    route = []
    for i in range(lax.axis_size(axis)):
        place = (i // stride) % count
        route.append((i, i + ((place + offset) % count - place) * stride))
    return lax.ppermute(block, axis, route)


def swap(block):
    return hop(block, "fsdp", 1, 2, 1)


def across(block):
    route = []
    for section in range(16):
        for group in range(16):
            to = (section ^ 1) * 16 + (group ^ 8)
            route.append((section * 16 + group, to))
    return lax.ppermute(block, ("section", "fsdp"), route)


def gather_pieces(shard):
    left = hop(shard, "fsdp", 2, 4, 1)
    right = hop(shard, "fsdp", 2, 4, -1)
    other = hop(shard, "fsdp", 8, 2, 1)
    far = hop(left, "fsdp", 2, 4, 1)
    other_left = hop(other, "fsdp", 2, 4, 1)
    other_right = hop(other, "fsdp", 2, 4, -1)
    other_far = hop(other_right, "fsdp", 2, 4, -1)
    near = [shard, left, right, other, far, other_left, other_right, other_far]
    return near + [swap(piece) for piece in near]


def gather_table(slab):
    half = slab.shape[0] // 2
    slab_swap = swap(slab)
    left = hop(slab, "fsdp", 2, 4, 1)
    right = hop(slab, "fsdp", 2, 4, -1)
    other = across(slab)
    far_a = hop(left[:half], "fsdp", 2, 4, 1)
    far_b = hop(right[half:], "fsdp", 2, 4, -1)
    other, slab_swap = lax.optimization_barrier((other, slab_swap))
    other_left = hop(other, "fsdp", 2, 4, 1)
    other_right = hop(other, "fsdp", 2, 4, -1)
    early = [swap(left), swap(right), swap(other)]
    far_a, far_b, early = lax.optimization_barrier((far_a, far_b, early))
    other_far = [across(far_a), across(far_b)]
    near = [slab, left, right, other, far_a, far_b, other_left, other_right] + other_far
    late = [swap(piece) for piece in near[4:]]
    return near + [slab_swap] + early + late


def places():
    me = lax.axis_index("fsdp")
    y, x, core = me // 8, (me // 2) % 4, me % 2
    steps = ((0, 0), (0, 3), (0, 1), (1, 0), (0, 2), (1, 3), (1, 1), (1, 2))
    found = []
    for c in (core, 1 - core):
        for i, o in steps:
            found.append(jnp.where(i == 0, y, 1 - y) * 8 + ((x + o) % 4) * 2 + c)
    return jnp.stack(found).astype(jnp.int32)


def gather_section(block):
    return lax.all_to_all(
        jnp.broadcast_to(block[None], (16,) + block.shape), "section", 0, 0, tiled=True
    )


def along_y(block):
    mate = hop(block, "section", 1, 2, 1)
    even = lax.axis_index("section") % 2 == 0
    return jnp.stack([jnp.where(even, block, mate), jnp.where(even, mate, block)])


def along_z(pair):
    planes = [list(range(y, 16, 2)) for y in range(2)]
    whole = lax.all_gather(pair, "section", axis=0, axis_index_groups=planes)
    return whole.reshape((16,) + pair.shape[1:])


def add(keep, got):
    return (keep.astype(F32) + got.astype(F32)).astype(BF16)


def among_chips(chunks):
    chips = [list(range(core, 16, 2)) for core in range(2)]
    return lax.all_to_all(chunks, "fsdp", 0, 0, tiled=True, axis_index_groups=chips)


def project(place_ref, x_ref, y_ref, *rest):
    pieces = rest[:16]
    out_ref, w_ref, xv_ref, yv_ref, sem = rest[16:]
    size, rank = pieces[0].shape[0], pieces[0].shape[1] // 2
    copies = [pltpu.make_async_copy(x_ref, xv_ref, sem.at[16])]
    for at, piece in enumerate(pieces):
        span = pl.ds(pl.multiple_of(place_ref[at] * size, size), size)
        copies.append(pltpu.make_async_copy(piece, w_ref.at[span, :], sem.at[at]))
    last = pltpu.make_async_copy(y_ref, yv_ref, sem.at[17])
    for copy in copies + [last]:
        copy.start()
    for copy in copies:
        copy.wait()
    out_ref[:, : 2 * rank] = dot(xv_ref[...], w_ref[...], NN).astype(BF16)
    last.wait()
    out_ref[:, 2 * rank :] = dot(yv_ref[...], w_ref[:, rank:], NN).astype(BF16)


def chain(width, s_ref, place_ref, a_hbm, norm_ref, *rest):
    pieces = rest[:20]
    pick_ref, keep_ref, send_ref = rest[20:23]
    z_ref, a_ref, w_ref, lift_ref, act_ref, slope_ref, inv_ref = rest[23:30]
    q_ref, p_ref, sq_ref, sums_ref, sem = rest[30:]
    layers = a_ref.shape[0]
    rank = z_ref.shape[2]
    cut = [slice(rank * i, rank * (i + 1)) for i in range(layers)]
    parts, many = 4, layers // 4
    first = pltpu.make_async_copy(a_hbm, a_ref, sem.at[parts, 0])
    first.start()
    copies = []
    for part in range(parts):
        some = pl.ds(part * many, many)
        for at, whole in enumerate((0, 1, 2, 3, None, 6, 7, None) * 2):
            first_of = 10 * (at // 8)
            if whole is not None:
                piece = pieces[first_of + whole].at[some]
            else:
                half = first_of + (4 if at % 8 == 4 else 8) + part // 2
                piece = pieces[half].at[pl.ds(part % 2 * many, many)]
            span = pl.ds(pl.multiple_of(place_ref[at] * rank, rank), rank)
            copy = pltpu.make_async_copy(piece, z_ref.at[some, span, :], sem.at[part, at])
            copy.start()
            copies.append(copy)
    first.wait()
    for s in range(layers):
        w_ref[s] = a_ref[s, :, cut[1]].astype(F32)
        lift_ref[s] = a_ref[s, :, cut[2]].astype(F32)
    scale = 1.0 / width
    total = norm_ref[...]
    for s in range(layers):
        if s % many == 0:
            for copy in copies[16 * (s // many) : 16 * (s // many) + 16]:
                copy.wait()
        inverse = lax.rsqrt(jnp.maximum(total, 0.0) * scale + 1e-05)
        raw = a_ref[s, :, cut[0]].astype(F32)
        if s > 0:
            raw = raw + dot(q_ref[:, : rank * s], z_ref[s, : rank * s, :], NN)
        act = raw * inverse
        sigma = jax.nn.sigmoid(act)
        now = (act * sigma).astype(BF16)
        q_ref[:, cut[s]] = now
        slope_ref[s] = sigma * (1.0 + act * (1.0 - sigma))
        act_ref[s] = act
        inv_ref[s] = jnp.broadcast_to(inverse, act.shape)
        wide = now.astype(F32)
        ahead = dot(now, z_ref[s, rank * s :, :], NT)
        own = ahead[:, :rank]
        here = w_ref[s]
        total = total + jnp.sum(wide * (2.0 * here + own), axis=1, keepdims=True)
        w_ref[s] = here + own
        for k in range(s + 1, layers):
            w_ref[k] += ahead[:, cut[k - s]]
    shrink = jnp.zeros_like(total)
    for s in range(layers - 1, -1, -1):
        up = lift_ref[s]
        if s + 1 < layers:
            up = up - shrink * w_ref[s]
            up = up - dot(sq_ref[:, rank * (s + 1) :], z_ref[s, rank * (s + 1) :, :], NN)
        grad = (up * slope_ref[s]).astype(BF16).astype(F32)
        inverse = inv_ref[s]
        now = (grad * inverse).astype(BF16)
        p_ref[:, cut[s]] = now
        sq_ref[:, cut[s]] = (shrink * q_ref[:, cut[s]].astype(F32)).astype(BF16)
        if s > 0:
            back = dot(now, z_ref[s, : rank * s, :], NT)
            for k in range(s):
                lift_ref[k] += back[:, cut[k]]
        mean = jnp.sum(grad * act_ref[s] * inverse * inverse, axis=1, keepdims=True) * scale
        shrink = shrink + mean
    here = pl.ds(pl.multiple_of(s_ref[0] * rank, rank), rank)
    p_t, q_t, sq_t = p_ref[:, here].T, q_ref[:, here].T, sq_ref[:, here].T
    both = jnp.concatenate([p_t, -sq_t], axis=0)
    pick_ref[: 2 * rank] = both
    pick_ref[2 * rank :] = q_t
    for j in range(layers):

        @pl.when(j < s_ref[0])
        def _():
            sums_ref[...] = dot(both, q_ref[:, cut[j]], NN).astype(BF16)

        @pl.when(j >= s_ref[0])
        def _():
            first = dot(q_t, p_ref[:, cut[j]], NN)
            first = jnp.where(j == s_ref[0], 0.0, first)
            sums_ref[:rank] = first.astype(BF16)
            sums_ref[rank:] = (-dot(q_t, sq_ref[:, cut[j]], NN)).astype(BF16)

        @pl.when(s_ref[1] == j % 2)
        def _():
            keep_ref[j // 2] = sums_ref[...]

        @pl.when(s_ref[1] != j % 2)
        def _():
            send_ref[j // 2] = sums_ref[...]


def chain_call(width, here, place, projected, norm, table):
    sections, tokens, wide = projected.shape
    rank = wide // 3
    smem = pl.BlockSpec(memory_space=pltpu.SMEM)
    vmem = pl.BlockSpec(memory_space=pltpu.VMEM)
    in_hbm = pl.BlockSpec(memory_space=pltpu.HBM)
    big = pltpu.VMEM((sections, tokens, rank), F32)
    flat = pltpu.VMEM((tokens, sections * rank), BF16)
    return pl.pallas_call(
        functools.partial(chain, width),
        out_shape=(
            jax.ShapeDtypeStruct((3 * rank, tokens), BF16),
            jax.ShapeDtypeStruct((8, 2 * rank, rank), BF16),
            jax.ShapeDtypeStruct((8, 2 * rank, rank), BF16),
        ),
        in_specs=[smem, smem, in_hbm, vmem] + [in_hbm] * 20,
        out_specs=(vmem,) * 3,
        scratch_shapes=[pltpu.VMEM((sections, sections * rank, rank), BF16)]
        + [pltpu.VMEM((sections, tokens, wide), BF16)]
        + [big] * 5
        + [flat] * 3
        + [pltpu.VMEM((2 * rank, rank), BF16), pltpu.SemaphoreType.DMA((5, 16))],
        compiler_params=pltpu.CompilerParams(vmem_limit_bytes=57 * MIB),
        cost_estimate=pl.CostEstimate(
            flops=2 * 10**10, bytes_accessed=12 * MIB, transcendentals=10**6
        ),
        name="chain",
    )(here, place, projected, norm, *table)


def outer(s_ref, pick_ref, x_hbm, y_hbm, keep_ref, send_ref, x_ref, y_ref, sem):
    rank = pick_ref.shape[0] // 3
    half, _, piece = keep_ref.shape
    first = s_ref[1] == 0
    copies = []
    for i in range(half):
        span = pl.ds(2 * piece * i, 2 * piece)
        for k, (far, near) in enumerate(((x_hbm, x_ref), (y_hbm, y_ref))):
            copies.append(pltpu.make_async_copy(far.at[:, span], near.at[:, span], sem.at[k, i]))
            copies[-1].start()
    for i in range(half):
        span = slice(2 * piece * i, 2 * piece * (i + 1))
        copies[2 * i].wait()
        copies[2 * i + 1].wait()
        from_x = dot(pick_ref[: 2 * rank], x_ref[:, span], NN)
        from_y = dot(pick_ref[2 * rank :], y_ref[:, span], NN)
        both = jnp.concatenate([from_x[:rank], from_x[rank:] + from_y], axis=0).astype(BF16)
        even, odd = both[:, :piece], both[:, piece:]
        keep_ref[i] = jnp.where(first, even, odd)
        send_ref[i] = jnp.where(first, odd, even)


def finish(s_ref, part_ref, mate_ref, up_hbm, down_hbm, own_ref, gain_ref, *rest):
    down_out, gain_out, up_out, up_ref, down_ref, sem = rest
    copies = [
        pltpu.make_async_copy(up_hbm, up_ref, sem.at[0]),
        pltpu.make_async_copy(down_hbm, down_ref, sem.at[1]),
    ]
    for copy in copies:
        copy.start()
    layers, rank, piece = up_ref.shape
    held = part_ref[0, :, :piece].astype(F32)
    for k in range(1, part_ref.shape[0]):
        held = held + part_ref[k, :, :piece].astype(F32)
    first = s_ref[1] == 0
    zero = jnp.zeros((rank, rank), BF16)
    masked, after = [], []
    for j in range(layers):
        ours, theirs = part_ref[j // 2, :, piece:], mate_ref[j // 2]
        sums = jnp.where(first == (j % 2 == 0), ours, theirs)
        before = jnp.where(j < s_ref[0], sums[:rank], zero)
        masked.append(jnp.concatenate([before, sums[rank:]], axis=0))
        after.append(jnp.where(j > s_ref[0], sums[:rank], zero))
    for copy in copies:
        copy.wait()
    held = held + dot(jnp.concatenate(masked, axis=1), up_ref[...].reshape(-1, piece), NN)
    held_up = held[rank:]
    for k in range(layers):
        held_up = held_up + dot(after[k], down_ref[k], NT)
    up_out[...] = held_up
    held_down = held[:rank]
    down_out[...] = (held_down * gain_ref[...]).T
    gain_out[...] = jnp.sum(own_ref[...].astype(F32).T * held_down, axis=0, keepdims=True)


def on_device(inputs, out_grad, down_proj, gain, up_proj):
    sections, groups = lax.axis_size("section"), lax.axis_size("fsdp")
    s = lax.axis_index("section")
    here = jnp.stack([s, lax.axis_index("fsdp") % 2]).astype(jnp.int32)
    place = places()
    width = inputs.shape[2]
    x = inputs.reshape(-1, width)
    y = out_grad.reshape(-1, width)
    tokens = x.shape[0]
    down, gain_row, up = down_proj[0], gain[0].astype(F32), up_proj[0]
    piece, rank = down.shape
    smem = pl.BlockSpec(memory_space=pltpu.SMEM)
    vmem = pl.BlockSpec(memory_space=pltpu.VMEM)
    in_hbm = pl.BlockSpec(memory_space=pltpu.HBM)

    scaled_down = (down.astype(F32) * gain_row[:, None]).astype(BF16)
    weights = jnp.concatenate([scaled_down, up.T], axis=1)
    up_all = along_z(along_y(up))

    projected = pl.pallas_call(
        project,
        out_shape=jax.ShapeDtypeStruct((tokens, 3 * rank), BF16),
        in_specs=[smem] + [in_hbm] * 18,
        out_specs=vmem,
        scratch_shapes=[
            pltpu.VMEM((width, 2 * rank), BF16),
            pltpu.VMEM(x.shape, BF16),
            pltpu.VMEM(y.shape, BF16),
            pltpu.SemaphoreType.DMA((18,)),
        ],
        compiler_params=pltpu.CompilerParams(vmem_limit_bytes=57 * MIB),
        name="project",
    )(place, x, y, *gather_pieces(weights))
    up_all, projected, late = lax.optimization_barrier(
        (up_all, projected, along_y(scaled_down))
    )
    projected = along_z(along_y(projected))
    norm = jnp.sum(jnp.square(x.astype(F32)), axis=1, keepdims=True)

    pairs = dot(up_all.reshape(sections * rank, piece), weights, NN)
    layer = lax.broadcasted_iota(jnp.int32, (sections * rank, 1), 0) // rank
    chosen = jnp.where(layer < s, pairs[:, :rank], pairs[:, rank:]).astype(BF16)
    chosen = lax.all_to_all(chosen.reshape(groups, rank, rank), "fsdp", 0, 0, tiled=True)
    block = jnp.sum(chosen.astype(F32), axis=0).astype(BF16)
    table = gather_table(gather_section(block))
    late, _ = lax.optimization_barrier((late, block))
    down_all = along_z(late)

    pick, cross, cross_out = chain_call(width, here, place, projected, norm, table)
    cross = add(cross, swap(cross_out))
    cross, pick = lax.optimization_barrier((cross, pick))
    cross = among_chips(cross)
    half = groups // 2
    part, part_out = pl.pallas_call(
        outer,
        out_shape=(jax.ShapeDtypeStruct((half, 2 * rank, piece), BF16),) * 2,
        in_specs=[smem, vmem, in_hbm, in_hbm],
        out_specs=(vmem,) * 2,
        scratch_shapes=[
            pltpu.VMEM(x.shape, BF16),
            pltpu.VMEM(y.shape, BF16),
            pltpu.SemaphoreType.DMA((2, half)),
        ],
        compiler_params=pltpu.CompilerParams(vmem_limit_bytes=57 * MIB),
        cost_estimate=pl.CostEstimate(
            flops=7 * 10**9, bytes_accessed=9 * MIB, transcendentals=0
        ),
        name="outer",
    )(here, pick, x, y)
    part_got = swap(part_out)
    cross = jnp.sum(cross.astype(F32), axis=0).astype(BF16)
    cross = jnp.broadcast_to(cross[None], (half, 2 * rank, rank))
    part = among_chips(jnp.concatenate([add(part, part_got), cross], axis=2))
    mate = swap(part[:, :, piece:])

    grad_down, grad_gain, grad_up = pl.pallas_call(
        finish,
        out_shape=(
            jax.ShapeDtypeStruct((piece, rank), F32),
            jax.ShapeDtypeStruct((1, piece), F32),
            jax.ShapeDtypeStruct((rank, piece), F32),
        ),
        in_specs=[smem, vmem, vmem, in_hbm, in_hbm, vmem, vmem],
        out_specs=(vmem,) * 3,
        scratch_shapes=[
            pltpu.VMEM(up_all.shape, BF16),
            pltpu.VMEM(down_all.shape, BF16),
            pltpu.SemaphoreType.DMA((2,)),
        ],
        compiler_params=pltpu.CompilerParams(vmem_limit_bytes=57 * MIB),
        name="finish",
    )(here, part, mate, up_all, down_all, down, gain_row[None])
    return (grad_down[None], grad_gain, grad_up[None])


def solution(mesh):
    placed = (
        P(None, "fsdp", None),
        P(None, "fsdp", None),
        P("section", "fsdp", None),
        P("section", "fsdp"),
        P("section", None, "fsdp"),
    )
    return jax.shard_map(
        on_device,
        mesh=mesh,
        in_specs=placed,
        out_specs=(P("section", "fsdp", None), P("section", "fsdp"), P("section", None, "fsdp")),
        check_vma=False,
    )
```

```python
import functools

import jax
import jax.numpy as jnp
from jax import lax
from jax.experimental import pallas as pl
from jax.experimental.pallas import tpu as pltpu
from jax.sharding import PartitionSpec as P

F32 = jnp.float32
BF16 = jnp.bfloat16
NN = ((1,), (0,))
NT = ((1,), (1,))
TN = ((0,), (0,))
MIB = 2**20


def dot(a, b, dims):
    return lax.dot_general(a, b, (dims, ((), ())), preferred_element_type=F32)


def hop(block, axis, stride, count, offset):
    route = []
    for i in range(lax.axis_size(axis)):
        place = (i // stride) % count
        route.append((i, i + ((place + offset) % count - place) * stride))
    return lax.ppermute(block, axis, route)


def swap(block):
    return hop(block, "fsdp", 1, 2, 1)


def across(block):
    route = []
    for section in range(16):
        for group in range(16):
            to = (section ^ 1) * 16 + (group ^ 8)
            route.append((section * 16 + group, to))
    return lax.ppermute(block, ("section", "fsdp"), route)


def gather_pieces(shard):
    left = hop(shard, "fsdp", 2, 4, 1)
    right = hop(shard, "fsdp", 2, 4, -1)
    other = hop(shard, "fsdp", 8, 2, 1)
    far = hop(left, "fsdp", 2, 4, 1)
    other_left = hop(other, "fsdp", 2, 4, 1)
    other_right = hop(other, "fsdp", 2, 4, -1)
    other_far = hop(other_right, "fsdp", 2, 4, -1)
    near = [shard, left, right, other, far, other_left, other_right, other_far]
    return near + [swap(piece) for piece in near]


def gather_table(slab):
    half = slab.shape[0] // 2
    slab_swap = swap(slab)
    left = hop(slab, "fsdp", 2, 4, 1)
    right = hop(slab, "fsdp", 2, 4, -1)
    other = across(slab)
    far_a = hop(left[:half], "fsdp", 2, 4, 1)
    far_b = hop(right[half:], "fsdp", 2, 4, -1)
    other, slab_swap = lax.optimization_barrier((other, slab_swap))
    other_left = hop(other, "fsdp", 2, 4, 1)
    other_right = hop(other, "fsdp", 2, 4, -1)
    early = [swap(left), swap(right), swap(other)]
    far_a, far_b, early = lax.optimization_barrier((far_a, far_b, early))
    other_far = [across(far_a), across(far_b)]
    near = [slab, left, right, other, far_a, far_b, other_left, other_right] + other_far
    late = [swap(piece) for piece in near[4:]]
    return near + [slab_swap] + early + late


def places():
    me = lax.axis_index("fsdp")
    y, x, core = me // 8, (me // 2) % 4, me % 2
    steps = ((0, 0), (0, 3), (0, 1), (1, 0), (0, 2), (1, 3), (1, 1), (1, 2))
    found = []
    for c in (core, 1 - core):
        for i, o in steps:
            found.append(jnp.where(i == 0, y, 1 - y) * 8 + ((x + o) % 4) * 2 + c)
    return jnp.stack(found).astype(jnp.int32)


def gather_section(block):
    return lax.all_to_all(
        jnp.broadcast_to(block[None], (16,) + block.shape), "section", 0, 0, tiled=True
    )


def along_y(block):
    mate = hop(block, "section", 1, 2, 1)
    even = lax.axis_index("section") % 2 == 0
    return jnp.stack([jnp.where(even, block, mate), jnp.where(even, mate, block)])


def along_z(pair):
    planes = [list(range(y, 16, 2)) for y in range(2)]
    whole = lax.all_gather(pair, "section", axis=0, axis_index_groups=planes)
    return whole.reshape((16,) + pair.shape[1:])


def add(keep, got):
    return (keep.astype(F32) + got.astype(F32)).astype(BF16)


def among_chips(chunks):
    chips = [list(range(core, 16, 2)) for core in range(2)]
    return lax.all_to_all(chunks, "fsdp", 0, 0, tiled=True, axis_index_groups=chips)


def project(place_ref, x_ref, y_ref, *rest):
    pieces = rest[:16]
    out_ref, w_ref, xv_ref, yv_ref, sem = rest[16:]
    size, rank = pieces[0].shape[0], pieces[0].shape[1] // 2
    copies = [pltpu.make_async_copy(x_ref, xv_ref, sem.at[16])]
    for at, piece in enumerate(pieces):
        span = pl.ds(pl.multiple_of(place_ref[at] * size, size), size)
        copies.append(pltpu.make_async_copy(piece, w_ref.at[span, :], sem.at[at]))
    last = pltpu.make_async_copy(y_ref, yv_ref, sem.at[17])
    for copy in copies + [last]:
        copy.start()
    for copy in copies:
        copy.wait()
    out_ref[:, : 2 * rank] = dot(xv_ref[...], w_ref[...], NN).astype(BF16)
    last.wait()
    out_ref[:, 2 * rank :] = dot(yv_ref[...], w_ref[:, rank:], NN).astype(BF16)


def chain(width, s_ref, place_ref, a_hbm, norm_ref, x_hbm, y_hbm, *rest):
    pieces = rest[:20]
    keep_ref, send_ref, keep_part, send_part = rest[20:24]
    z_ref, a_ref, w_ref, lift_ref, act_ref, slope_ref, inv_ref = rest[24:31]
    q_ref, p_ref, sq_ref, sums_ref, x_ref, y_ref, sem = rest[31:]
    layers = a_ref.shape[0]
    rank = z_ref.shape[2]
    cut = [slice(rank * i, rank * (i + 1)) for i in range(layers)]
    parts, many = 4, layers // 4
    first = pltpu.make_async_copy(a_hbm, a_ref, sem.at[parts, 0])
    first.start()
    copies = []
    for part in range(parts):
        some = pl.ds(part * many, many)
        for at, whole in enumerate((0, 1, 2, 3, None, 6, 7, None) * 2):
            first_of = 10 * (at // 8)
            if whole is not None:
                piece = pieces[first_of + whole].at[some]
            else:
                half = first_of + (4 if at % 8 == 4 else 8) + part // 2
                piece = pieces[half].at[pl.ds(part % 2 * many, many)]
            span = pl.ds(pl.multiple_of(place_ref[at] * rank, rank), rank)
            copy = pltpu.make_async_copy(piece, z_ref.at[some, span, :], sem.at[part, at])
            copy.start()
            copies.append(copy)
    whole = [
        pltpu.make_async_copy(x_hbm, x_ref, sem.at[parts, 1]),
        pltpu.make_async_copy(y_hbm, y_ref, sem.at[parts, 2]),
    ]
    for copy in whole:
        copy.start()
    first.wait()
    for s in range(layers):
        w_ref[s] = a_ref[s, :, cut[1]].astype(F32)
        lift_ref[s] = a_ref[s, :, cut[2]].astype(F32)
    scale = 1.0 / width
    total = norm_ref[...]
    for s in range(layers):
        if s % many == 0:
            for copy in copies[16 * (s // many) : 16 * (s // many) + 16]:
                copy.wait()
        inverse = lax.rsqrt(jnp.maximum(total, 0.0) * scale + 1e-05)
        raw = a_ref[s, :, cut[0]].astype(F32)
        if s > 0:
            raw = raw + dot(q_ref[:, : rank * s], z_ref[s, : rank * s, :], NN)
        act = raw * inverse
        sigma = jax.nn.sigmoid(act)
        now = (act * sigma).astype(BF16)
        q_ref[:, cut[s]] = now
        slope_ref[s] = sigma * (1.0 + act * (1.0 - sigma))
        act_ref[s] = act
        inv_ref[s] = jnp.broadcast_to(inverse, act.shape)
        wide = now.astype(F32)
        ahead = dot(now, z_ref[s, rank * s :, :], NT)
        own = ahead[:, :rank]
        here = w_ref[s]
        total = total + jnp.sum(wide * (2.0 * here + own), axis=1, keepdims=True)
        w_ref[s] = here + own
        for k in range(s + 1, layers):
            w_ref[k] += ahead[:, cut[k - s]]
    shrink = jnp.zeros_like(total)
    for s in range(layers - 1, -1, -1):
        up = lift_ref[s]
        if s + 1 < layers:
            up = up - shrink * w_ref[s]
            up = up - dot(sq_ref[:, rank * (s + 1) :], z_ref[s, rank * (s + 1) :, :], NN)
        grad = (up * slope_ref[s]).astype(BF16).astype(F32)
        inverse = inv_ref[s]
        now = (grad * inverse).astype(BF16)
        p_ref[:, cut[s]] = now
        sq_ref[:, cut[s]] = (shrink * q_ref[:, cut[s]].astype(F32)).astype(BF16)
        if s > 0:
            back = dot(now, z_ref[s, : rank * s, :], NT)
            for k in range(s):
                lift_ref[k] += back[:, cut[k]]
        mean = jnp.sum(grad * act_ref[s] * inverse * inverse, axis=1, keepdims=True) * scale
        shrink = shrink + mean
    here = pl.ds(pl.multiple_of(s_ref[0] * rank, rank), rank)
    p_t, q_t, sq_t = p_ref[:, here].T, q_ref[:, here].T, sq_ref[:, here].T
    both = jnp.concatenate([p_t, -sq_t], axis=0)
    for j in range(layers):

        @pl.when(j < s_ref[0])
        def _():
            sums_ref[...] = dot(both, q_ref[:, cut[j]], NN).astype(BF16)

        @pl.when(j >= s_ref[0])
        def _():
            first = dot(q_t, p_ref[:, cut[j]], NN)
            first = jnp.where(j == s_ref[0], 0.0, first)
            sums_ref[:rank] = first.astype(BF16)
            sums_ref[rank:] = (-dot(q_t, sq_ref[:, cut[j]], NN)).astype(BF16)

        @pl.when(s_ref[1] == j % 2)
        def _():
            keep_ref[j // 2] = sums_ref[...]

        @pl.when(s_ref[1] != j % 2)
        def _():
            send_ref[j // 2] = sums_ref[...]

    for copy in whole:
        copy.wait()
    half, _, piece = keep_part.shape
    even_core = s_ref[1] == 0
    for i in range(half):
        span = slice(2 * piece * i, 2 * piece * (i + 1))
        from_x = dot(both, x_ref[:, span], NN)
        from_y = dot(q_t, y_ref[:, span], NN)
        sums = jnp.concatenate([from_x[:rank], from_x[rank:] + from_y], axis=0).astype(BF16)
        even, odd = sums[:, :piece], sums[:, piece:]
        keep_part[i] = jnp.where(even_core, even, odd)
        send_part[i] = jnp.where(even_core, odd, even)


def chain_call(here, place, projected, norm, x, y, table):
    sections, tokens, wide = projected.shape
    rank, width, piece = wide // 3, x.shape[1], x.shape[1] // 16
    smem = pl.BlockSpec(memory_space=pltpu.SMEM)
    vmem = pl.BlockSpec(memory_space=pltpu.VMEM)
    in_hbm = pl.BlockSpec(memory_space=pltpu.HBM)
    big = pltpu.VMEM((sections, tokens, rank), F32)
    flat = pltpu.VMEM((tokens, sections * rank), BF16)
    return pl.pallas_call(
        functools.partial(chain, width),
        out_shape=(
            jax.ShapeDtypeStruct((8, 2 * rank, rank), BF16),
            jax.ShapeDtypeStruct((8, 2 * rank, rank), BF16),
            jax.ShapeDtypeStruct((8, 2 * rank, piece), BF16),
            jax.ShapeDtypeStruct((8, 2 * rank, piece), BF16),
        ),
        in_specs=[smem, smem, in_hbm, vmem] + [in_hbm] * 22,
        out_specs=(vmem,) * 4,
        scratch_shapes=[pltpu.VMEM((sections, sections * rank, rank), BF16)]
        + [pltpu.VMEM((sections, tokens, wide), BF16)]
        + [big] * 5
        + [flat] * 3
        + [pltpu.VMEM((2 * rank, rank), BF16)]
        + [pltpu.VMEM(x.shape, BF16)] * 2
        + [pltpu.SemaphoreType.DMA((5, 16))],
        compiler_params=pltpu.CompilerParams(vmem_limit_bytes=57 * MIB),
        cost_estimate=pl.CostEstimate(
            flops=2 * 10**10, bytes_accessed=12 * MIB, transcendentals=10**6
        ),
        name="chain",
    )(here, place, projected, norm, x, y, *table)


def finish(s_ref, part_ref, mate_ref, up_hbm, down_hbm, own_ref, gain_ref, *rest):
    down_out, gain_out, up_out, up_ref, down_ref, sem = rest
    copies = [
        pltpu.make_async_copy(up_hbm, up_ref, sem.at[0]),
        pltpu.make_async_copy(down_hbm, down_ref, sem.at[1]),
    ]
    for copy in copies:
        copy.start()
    layers, rank, piece = up_ref.shape
    held = part_ref[0, :, :piece].astype(F32)
    for k in range(1, part_ref.shape[0]):
        held = held + part_ref[k, :, :piece].astype(F32)
    first = s_ref[1] == 0
    zero = jnp.zeros((rank, rank), BF16)
    masked, after = [], []
    for j in range(layers):
        ours, theirs = part_ref[j // 2, :, piece:], mate_ref[j // 2]
        sums = jnp.where(first == (j % 2 == 0), ours, theirs)
        before = jnp.where(j < s_ref[0], sums[:rank], zero)
        masked.append(jnp.concatenate([before, sums[rank:]], axis=0))
        after.append(jnp.where(j > s_ref[0], sums[:rank], zero))
    for copy in copies:
        copy.wait()
    held = held + dot(jnp.concatenate(masked, axis=1), up_ref[...].reshape(-1, piece), NN)
    held_up = held[rank:]
    for k in range(layers):
        held_up = held_up + dot(after[k], down_ref[k], NT)
    up_out[...] = held_up
    held_down = held[:rank]
    down_out[...] = (held_down * gain_ref[...]).T
    gain_out[...] = jnp.sum(own_ref[...].astype(F32).T * held_down, axis=0, keepdims=True)


def on_device(inputs, out_grad, down_proj, gain, up_proj):
    sections, groups = lax.axis_size("section"), lax.axis_size("fsdp")
    s = lax.axis_index("section")
    here = jnp.stack([s, lax.axis_index("fsdp") % 2]).astype(jnp.int32)
    place = places()
    width = inputs.shape[2]
    x = inputs.reshape(-1, width)
    y = out_grad.reshape(-1, width)
    tokens = x.shape[0]
    down, gain_row, up = down_proj[0], gain[0].astype(F32), up_proj[0]
    piece, rank = down.shape
    smem = pl.BlockSpec(memory_space=pltpu.SMEM)
    vmem = pl.BlockSpec(memory_space=pltpu.VMEM)
    in_hbm = pl.BlockSpec(memory_space=pltpu.HBM)

    scaled_down = (down.astype(F32) * gain_row[:, None]).astype(BF16)
    weights = jnp.concatenate([scaled_down, up.T], axis=1)

    up_all = along_z(along_y(up))

    projected = pl.pallas_call(
        project,
        out_shape=jax.ShapeDtypeStruct((tokens, 3 * rank), BF16),
        in_specs=[smem] + [in_hbm] * 18,
        out_specs=vmem,
        scratch_shapes=[
            pltpu.VMEM((width, 2 * rank), BF16),
            pltpu.VMEM(x.shape, BF16),
            pltpu.VMEM(y.shape, BF16),
            pltpu.SemaphoreType.DMA((18,)),
        ],
        compiler_params=pltpu.CompilerParams(vmem_limit_bytes=57 * MIB),
        cost_estimate=pl.CostEstimate(
            flops=8 * 10**9, bytes_accessed=9 * MIB, transcendentals=0
        ),
        name="project",
    )(place, x, y, *gather_pieces(weights))
    up_all, pair, late = lax.optimization_barrier(
        (up_all, along_y(projected), along_y(scaled_down))
    )
    projected = along_z(pair)
    norm = jnp.sum(jnp.square(x.astype(F32)), axis=1, keepdims=True)

    pairs = dot(up_all.reshape(sections * rank, piece), weights, NN)
    layer = lax.broadcasted_iota(jnp.int32, (sections * rank, 1), 0) // rank
    chosen = jnp.where(layer < s, pairs[:, :rank], pairs[:, rank:]).astype(BF16)
    chosen = chosen.reshape(groups, rank, rank)
    chosen = lax.all_to_all(chosen, "fsdp", 0, 0, tiled=True)
    block = jnp.sum(chosen.astype(F32), axis=0).astype(BF16)
    block, late = lax.optimization_barrier((block, late))
    table = gather_table(gather_section(block))
    down_all = along_z(late)

    cross, cross_out, part, part_out = chain_call(here, place, projected, norm, x, y, table)
    cross_got, part_out = lax.optimization_barrier((swap(cross_out), part_out))
    cross = among_chips(add(cross, cross_got))
    part_got = swap(part_out)
    cross = jnp.sum(cross.astype(F32), axis=0).astype(BF16)
    half = groups // 2
    cross = jnp.broadcast_to(cross[None], (half, 2 * rank, rank))
    part = among_chips(jnp.concatenate([add(part, part_got), cross], axis=2))
    mate = swap(part[:, :, piece:])

    grad_down, grad_gain, grad_up = pl.pallas_call(
        finish,
        out_shape=(
            jax.ShapeDtypeStruct((piece, rank), F32),
            jax.ShapeDtypeStruct((1, piece), F32),
            jax.ShapeDtypeStruct((rank, piece), F32),
        ),
        in_specs=[smem, vmem, vmem, in_hbm, in_hbm, vmem, vmem],
        out_specs=(vmem,) * 3,
        scratch_shapes=[
            pltpu.VMEM(up_all.shape, BF16),
            pltpu.VMEM(down_all.shape, BF16),
            pltpu.SemaphoreType.DMA((2,)),
        ],
        compiler_params=pltpu.CompilerParams(vmem_limit_bytes=57 * MIB),
        name="finish",
    )(here, part, mate, up_all, down_all, down, gain_row[None])
    return (grad_down[None], grad_gain, grad_up[None])


def solution(mesh):
    placed = (
        P(None, "fsdp", None),
        P(None, "fsdp", None),
        P("section", "fsdp", None),
        P("section", "fsdp"),
        P("section", None, "fsdp"),
    )
    return jax.shard_map(
        on_device,
        mesh=mesh,
        in_specs=placed,
        out_specs=(P("section", "fsdp", None), P("section", "fsdp"), P("section", None, "fsdp")),
        check_vma=False,
    )
```

```python
import functools

import jax
import jax.numpy as jnp
from jax import lax
from jax.experimental import pallas as pl
from jax.experimental.pallas import tpu as pltpu
from jax.sharding import PartitionSpec as P

F32 = jnp.float32
BF16 = jnp.bfloat16
NN = ((1,), (0,))
NT = ((1,), (1,))
TN = ((0,), (0,))
MIB = 2**20


def dot(a, b, dims):
    return lax.dot_general(a, b, (dims, ((), ())), preferred_element_type=F32)


def hop(block, axis, stride, count, offset):
    route = []
    for i in range(lax.axis_size(axis)):
        place = (i // stride) % count
        route.append((i, i + ((place + offset) % count - place) * stride))
    return lax.ppermute(block, axis, route)


def swap(block):
    return hop(block, "fsdp", 1, 2, 1)


def across(block):
    route = []
    for section in range(16):
        for group in range(16):
            to = (section ^ 1) * 16 + (group ^ 8)
            route.append((section * 16 + group, to))
    return lax.ppermute(block, ("section", "fsdp"), route)


def gather_pieces(shard):
    left = hop(shard, "fsdp", 2, 4, 1)
    right = hop(shard, "fsdp", 2, 4, -1)
    other = hop(shard, "fsdp", 8, 2, 1)
    far = hop(left, "fsdp", 2, 4, 1)
    other_left = hop(other, "fsdp", 2, 4, 1)
    other_right = hop(other, "fsdp", 2, 4, -1)
    other_far = hop(other_right, "fsdp", 2, 4, -1)
    near = [shard, left, right, other, far, other_left, other_right, other_far]
    return near + [swap(piece) for piece in near]


def gather_table(slab):
    half = slab.shape[0] // 2
    slab_swap = swap(slab)
    left = hop(slab, "fsdp", 2, 4, 1)
    right = hop(slab, "fsdp", 2, 4, -1)
    other = across(slab)
    far_a = hop(left[:half], "fsdp", 2, 4, 1)
    far_b = hop(right[half:], "fsdp", 2, 4, -1)
    other, slab_swap = lax.optimization_barrier((other, slab_swap))
    other_left = hop(other, "fsdp", 2, 4, 1)
    other_right = hop(other, "fsdp", 2, 4, -1)
    early = [swap(left), swap(right), swap(other)]
    far_a, far_b, early = lax.optimization_barrier((far_a, far_b, early))
    other_far = [across(far_a), across(far_b)]
    near = [slab, left, right, other, far_a, far_b, other_left, other_right] + other_far
    late = [swap(piece) for piece in near[4:]]
    return near + [slab_swap] + early + late


def places():
    me = lax.axis_index("fsdp")
    y, x, core = me // 8, (me // 2) % 4, me % 2
    steps = ((0, 0), (0, 3), (0, 1), (1, 0), (0, 2), (1, 3), (1, 1), (1, 2))
    found = []
    for c in (core, 1 - core):
        for i, o in steps:
            found.append(jnp.where(i == 0, y, 1 - y) * 8 + ((x + o) % 4) * 2 + c)
    return jnp.stack(found).astype(jnp.int32)


def gather_section(block):
    return lax.all_to_all(
        jnp.broadcast_to(block[None], (16,) + block.shape), "section", 0, 0, tiled=True
    )


def along_y(block):
    mate = hop(block, "section", 1, 2, 1)
    even = lax.axis_index("section") % 2 == 0
    return jnp.stack([jnp.where(even, block, mate), jnp.where(even, mate, block)])


def along_z(pair):
    planes = [list(range(y, 16, 2)) for y in range(2)]
    whole = lax.all_gather(pair, "section", axis=0, axis_index_groups=planes)
    return whole.reshape((16,) + pair.shape[1:])


def add(keep, got):
    return (keep.astype(F32) + got.astype(F32)).astype(BF16)


def among_chips(chunks):
    chips = [list(range(core, 16, 2)) for core in range(2)]
    return lax.all_to_all(chunks, "fsdp", 0, 0, tiled=True, axis_index_groups=chips)


def project(place_ref, x_ref, y_ref, *rest):
    pieces = rest[:16]
    out_ref, w_ref, xv_ref, yv_ref, sem = rest[16:]
    size, rank = pieces[0].shape[0], pieces[0].shape[1] // 2
    copies = [pltpu.make_async_copy(x_ref, xv_ref, sem.at[16])]
    for at, piece in enumerate(pieces):
        span = pl.ds(pl.multiple_of(place_ref[at] * size, size), size)
        copies.append(pltpu.make_async_copy(piece, w_ref.at[span, :], sem.at[at]))
    last = pltpu.make_async_copy(y_ref, yv_ref, sem.at[17])
    for copy in copies + [last]:
        copy.start()
    for copy in copies:
        copy.wait()
    out_ref[:, : 2 * rank] = dot(xv_ref[...], w_ref[...], NN).astype(BF16)
    last.wait()
    out_ref[:, 2 * rank :] = dot(yv_ref[...], w_ref[:, rank:], NN).astype(BF16)


def chain(width, s_ref, place_ref, a_hbm, norm_ref, x_hbm, y_hbm, *rest):
    pieces = rest[:20]
    keep_ref, send_ref, keep_part, send_part = rest[20:24]
    z_ref, a_ref, w_ref, lift_ref, act_ref, slope_ref, inv_ref = rest[24:31]
    q_ref, p_ref, sq_ref, x_ref, y_ref, sem = rest[31:]
    layers = a_ref.shape[0]
    rank = z_ref.shape[2]
    cut = [slice(rank * i, rank * (i + 1)) for i in range(layers)]
    parts, many = 4, layers // 4
    first = pltpu.make_async_copy(a_hbm, a_ref, sem.at[parts, 0])
    first.start()
    copies = []
    for part in range(parts):
        some = pl.ds(part * many, many)
        for at, whole in enumerate((0, 1, 2, 3, None, 6, 7, None) * 2):
            first_of = 10 * (at // 8)
            if whole is not None:
                piece = pieces[first_of + whole].at[some]
            else:
                half = first_of + (4 if at % 8 == 4 else 8) + part // 2
                piece = pieces[half].at[pl.ds(part % 2 * many, many)]
            span = pl.ds(pl.multiple_of(place_ref[at] * rank, rank), rank)
            copy = pltpu.make_async_copy(piece, z_ref.at[some, span, :], sem.at[part, at])
            copy.start()
            copies.append(copy)
    whole = [
        pltpu.make_async_copy(x_hbm, x_ref, sem.at[parts, 1]),
        pltpu.make_async_copy(y_hbm, y_ref, sem.at[parts, 2]),
    ]
    for copy in whole:
        copy.start()
    first.wait()
    for s in range(layers):
        w_ref[s] = a_ref[s, :, cut[1]].astype(F32)
        lift_ref[s] = a_ref[s, :, cut[2]].astype(F32)
    scale = 1.0 / width
    total = norm_ref[...]
    for s in range(layers):
        if s % many == 0:
            for copy in copies[16 * (s // many) : 16 * (s // many) + 16]:
                copy.wait()
        inverse = lax.rsqrt(jnp.maximum(total, 0.0) * scale + 1e-05)
        raw = a_ref[s, :, cut[0]].astype(F32)
        if s > 0:
            raw = raw + dot(q_ref[:, : rank * s], z_ref[s, : rank * s, :], NN)
        act = raw * inverse
        sigma = jax.nn.sigmoid(act)
        now = (act * sigma).astype(BF16)
        q_ref[:, cut[s]] = now
        slope_ref[s] = sigma * (1.0 + act * (1.0 - sigma))
        act_ref[s] = act
        inv_ref[s] = jnp.broadcast_to(inverse, act.shape)
        wide = now.astype(F32)
        ahead = dot(now, z_ref[s, rank * s :, :], NT)
        own = ahead[:, :rank]
        here = w_ref[s]
        total = total + jnp.sum(wide * (2.0 * here + own), axis=1, keepdims=True)
        w_ref[s] = here + own
        for k in range(s + 1, layers):
            w_ref[k] += ahead[:, cut[k - s]]
    shrink = jnp.zeros_like(total)
    for s in range(layers - 1, -1, -1):
        up = lift_ref[s]
        if s + 1 < layers:
            up = up - shrink * w_ref[s]
            up = up - dot(sq_ref[:, rank * (s + 1) :], z_ref[s, rank * (s + 1) :, :], NN)
        grad = (up * slope_ref[s]).astype(BF16).astype(F32)
        inverse = inv_ref[s]
        now = (grad * inverse).astype(BF16)
        p_ref[:, cut[s]] = now
        sq_ref[:, cut[s]] = (shrink * q_ref[:, cut[s]].astype(F32)).astype(BF16)
        if s > 0:
            back = dot(now, z_ref[s, : rank * s, :], NT)
            for k in range(s):
                lift_ref[k] += back[:, cut[k]]
        mean = jnp.sum(grad * act_ref[s] * inverse * inverse, axis=1, keepdims=True) * scale
        shrink = shrink + mean
    here = pl.ds(pl.multiple_of(s_ref[0] * rank, rank), rank)
    p_t, q_t, sq_t = p_ref[:, here].T, q_ref[:, here].T, sq_ref[:, here].T
    both = jnp.concatenate([p_t, -sq_t], axis=0)
    even_core = s_ref[1] == 0
    for i in range(layers // 2):
        span = slice(2 * rank * i, 2 * rank * (i + 1))
        before = dot(both, q_ref[:, span], NN)
        after = dot(q_t, p_ref[:, span], NN)
        scaled = -dot(q_t, sq_ref[:, span], NN)
        found = []
        for k in range(2):
            j, some = 2 * i + k, slice(rank * k, rank * (k + 1))
            later = jnp.where(j == s_ref[0], 0.0, after[:, some])
            later = jnp.concatenate([later, scaled[:, some]], axis=0)
            found.append(jnp.where(j < s_ref[0], before[:, some], later).astype(BF16))
        keep_ref[i] = jnp.where(even_core, found[0], found[1])
        send_ref[i] = jnp.where(even_core, found[1], found[0])

    for copy in whole:
        copy.wait()
    half, _, piece = keep_part.shape
    for i in range(half):
        span = slice(2 * piece * i, 2 * piece * (i + 1))
        from_x = dot(both, x_ref[:, span], NN)
        from_y = dot(q_t, y_ref[:, span], NN)
        sums = jnp.concatenate([from_x[:rank], from_x[rank:] + from_y], axis=0).astype(BF16)
        even, odd = sums[:, :piece], sums[:, piece:]
        keep_part[i] = jnp.where(even_core, even, odd)
        send_part[i] = jnp.where(even_core, odd, even)


def chain_call(here, place, projected, norm, x, y, table):
    sections, tokens, wide = projected.shape
    rank, width, piece = wide // 3, x.shape[1], x.shape[1] // 16
    smem = pl.BlockSpec(memory_space=pltpu.SMEM)
    vmem = pl.BlockSpec(memory_space=pltpu.VMEM)
    in_hbm = pl.BlockSpec(memory_space=pltpu.HBM)
    big = pltpu.VMEM((sections, tokens, rank), F32)
    flat = pltpu.VMEM((tokens, sections * rank), BF16)
    return pl.pallas_call(
        functools.partial(chain, width),
        out_shape=(
            jax.ShapeDtypeStruct((8, 2 * rank, rank), BF16),
            jax.ShapeDtypeStruct((8, 2 * rank, rank), BF16),
            jax.ShapeDtypeStruct((8, 2 * rank, piece), BF16),
            jax.ShapeDtypeStruct((8, 2 * rank, piece), BF16),
        ),
        in_specs=[smem, smem, in_hbm, vmem] + [in_hbm] * 22,
        out_specs=(vmem,) * 4,
        scratch_shapes=[pltpu.VMEM((sections, sections * rank, rank), BF16)]
        + [pltpu.VMEM((sections, tokens, wide), BF16)]
        + [big] * 5
        + [flat] * 3
        + [pltpu.VMEM(x.shape, BF16)] * 2
        + [pltpu.SemaphoreType.DMA((5, 16))],
        compiler_params=pltpu.CompilerParams(vmem_limit_bytes=57 * MIB),
        cost_estimate=pl.CostEstimate(
            flops=2 * 10**10, bytes_accessed=12 * MIB, transcendentals=10**6
        ),
        name="chain",
    )(here, place, projected, norm, x, y, *table)


def finish(s_ref, part_ref, mate_ref, up_hbm, down_hbm, own_ref, gain_ref, *rest):
    down_out, gain_out, up_out, up_ref, down_ref, sem = rest
    copies = [
        pltpu.make_async_copy(up_hbm, up_ref, sem.at[0]),
        pltpu.make_async_copy(down_hbm, down_ref, sem.at[1]),
    ]
    for copy in copies:
        copy.start()
    layers, rank, piece = up_ref.shape
    held = part_ref[0, :, :piece].astype(F32)
    for k in range(1, part_ref.shape[0]):
        held = held + part_ref[k, :, :piece].astype(F32)
    first = s_ref[1] == 0
    zero = jnp.zeros((rank, rank), BF16)
    masked, after = [], []
    for j in range(layers):
        ours, theirs = part_ref[j // 2, :, piece:], mate_ref[j // 2]
        sums = jnp.where(first == (j % 2 == 0), ours, theirs)
        before = jnp.where(j < s_ref[0], sums[:rank], zero)
        masked.append(jnp.concatenate([before, sums[rank:]], axis=0))
        after.append(jnp.where(j > s_ref[0], sums[:rank], zero))
    for copy in copies:
        copy.wait()
    held = held + dot(jnp.concatenate(masked, axis=1), up_ref[...].reshape(-1, piece), NN)
    held_up = held[rank:]
    for k in range(layers):
        held_up = held_up + dot(after[k], down_ref[k], NT)
    up_out[...] = held_up
    held_down = held[:rank]
    down_out[...] = (held_down * gain_ref[...]).T
    gain_out[...] = jnp.sum(own_ref[...].astype(F32).T * held_down, axis=0, keepdims=True)


def on_device(inputs, out_grad, down_proj, gain, up_proj):
    sections, groups = lax.axis_size("section"), lax.axis_size("fsdp")
    s = lax.axis_index("section")
    here = jnp.stack([s, lax.axis_index("fsdp") % 2]).astype(jnp.int32)
    place = places()
    width = inputs.shape[2]
    x = inputs.reshape(-1, width)
    y = out_grad.reshape(-1, width)
    tokens = x.shape[0]
    down, gain_row, up = down_proj[0], gain[0].astype(F32), up_proj[0]
    piece, rank = down.shape
    smem = pl.BlockSpec(memory_space=pltpu.SMEM)
    vmem = pl.BlockSpec(memory_space=pltpu.VMEM)
    in_hbm = pl.BlockSpec(memory_space=pltpu.HBM)

    scaled_down = (down.astype(F32) * gain_row[:, None]).astype(BF16)
    weights = jnp.concatenate([scaled_down, up.T], axis=1)

    up_all = along_z(along_y(up))

    projected = pl.pallas_call(
        project,
        out_shape=jax.ShapeDtypeStruct((tokens, 3 * rank), BF16),
        in_specs=[smem] + [in_hbm] * 18,
        out_specs=vmem,
        scratch_shapes=[
            pltpu.VMEM((width, 2 * rank), BF16),
            pltpu.VMEM(x.shape, BF16),
            pltpu.VMEM(y.shape, BF16),
            pltpu.SemaphoreType.DMA((18,)),
        ],
        compiler_params=pltpu.CompilerParams(vmem_limit_bytes=57 * MIB),
        cost_estimate=pl.CostEstimate(
            flops=8 * 10**9, bytes_accessed=9 * MIB, transcendentals=0
        ),
        name="project",
    )(place, x, y, *gather_pieces(weights))
    up_all, pair, late = lax.optimization_barrier(
        (up_all, along_y(projected), along_y(scaled_down))
    )
    projected = along_z(pair)
    norm = jnp.sum(jnp.square(x.astype(F32)), axis=1, keepdims=True)

    pairs = dot(up_all.reshape(sections * rank, piece), weights, NN)
    layer = lax.broadcasted_iota(jnp.int32, (sections * rank, 1), 0) // rank
    chosen = jnp.where(layer < s, pairs[:, :rank], pairs[:, rank:]).astype(BF16)
    chosen = chosen.reshape(groups, rank, rank)
    chosen = lax.all_to_all(chosen, "fsdp", 0, 0, tiled=True)
    block = jnp.sum(chosen.astype(F32), axis=0).astype(BF16)
    block, late = lax.optimization_barrier((block, late))
    table = gather_table(gather_section(block))
    down_all = along_z(late)

    cross, cross_out, part, part_out = chain_call(here, place, projected, norm, x, y, table)
    cross_got, part_out = lax.optimization_barrier((swap(cross_out), part_out))
    cross = among_chips(add(cross, cross_got))
    part_got = swap(part_out)
    cross = jnp.sum(cross.astype(F32), axis=0).astype(BF16)
    half = groups // 2
    cross = jnp.broadcast_to(cross[None], (half, 2 * rank, rank))
    part = among_chips(jnp.concatenate([add(part, part_got), cross], axis=2))
    mate = swap(part[:, :, piece:])

    grad_down, grad_gain, grad_up = pl.pallas_call(
        finish,
        out_shape=(
            jax.ShapeDtypeStruct((piece, rank), F32),
            jax.ShapeDtypeStruct((1, piece), F32),
            jax.ShapeDtypeStruct((rank, piece), F32),
        ),
        in_specs=[smem, vmem, vmem, in_hbm, in_hbm, vmem, vmem],
        out_specs=(vmem,) * 3,
        scratch_shapes=[
            pltpu.VMEM(up_all.shape, BF16),
            pltpu.VMEM(down_all.shape, BF16),
            pltpu.SemaphoreType.DMA((2,)),
        ],
        compiler_params=pltpu.CompilerParams(vmem_limit_bytes=57 * MIB),
        name="finish",
    )(here, part, mate, up_all, down_all, down, gain_row[None])
    return (grad_down[None], grad_gain, grad_up[None])


def solution(mesh):
    placed = (
        P(None, "fsdp", None),
        P(None, "fsdp", None),
        P("section", "fsdp", None),
        P("section", "fsdp"),
        P("section", None, "fsdp"),
    )
    return jax.shard_map(
        on_device,
        mesh=mesh,
        in_specs=placed,
        out_specs=(P("section", "fsdp", None), P("section", "fsdp"), P("section", None, "fsdp")),
        check_vma=False,
    )
```

```python
import functools

import jax
import jax.numpy as jnp
from jax import lax
from jax.experimental import pallas as pl
from jax.experimental.pallas import tpu as pltpu
from jax.sharding import PartitionSpec as P

F32 = jnp.float32
BF16 = jnp.bfloat16
NN = ((1,), (0,))
NT = ((1,), (1,))
TN = ((0,), (0,))
MIB = 2**20


def dot(a, b, dims):
    return lax.dot_general(a, b, (dims, ((), ())), preferred_element_type=F32)


def hop(block, axis, stride, count, offset):
    route = []
    for i in range(lax.axis_size(axis)):
        place = (i // stride) % count
        route.append((i, i + ((place + offset) % count - place) * stride))
    return lax.ppermute(block, axis, route)


def swap(block):
    return hop(block, "fsdp", 1, 2, 1)


def across(block):
    route = []
    for section in range(16):
        for group in range(16):
            to = (section ^ 1) * 16 + (group ^ 8)
            route.append((section * 16 + group, to))
    return lax.ppermute(block, ("section", "fsdp"), route)


def gather_pieces(shard):
    left = hop(shard, "fsdp", 2, 4, 1)
    right = hop(shard, "fsdp", 2, 4, -1)
    other = hop(shard, "fsdp", 8, 2, 1)
    far = hop(left, "fsdp", 2, 4, 1)
    other_left = hop(other, "fsdp", 2, 4, 1)
    other_right = hop(other, "fsdp", 2, 4, -1)
    other_far = hop(other_right, "fsdp", 2, 4, -1)
    near = [shard, left, right, other, far, other_left, other_right, other_far]
    return near + [swap(piece) for piece in near]


def gather_table(slab, norm):
    half = slab.shape[0] // 2
    slab_swap = swap(slab)
    left = hop(slab, "fsdp", 2, 4, 1)
    right = hop(slab, "fsdp", 2, 4, -1)
    other = across(slab)
    far_a = hop(left[:half], "fsdp", 2, 4, 1)
    far_b = hop(right[half:], "fsdp", 2, 4, -1)
    other, slab_swap, norm = lax.optimization_barrier((other, slab_swap, norm))
    other_left = hop(other, "fsdp", 2, 4, 1)
    other_right = hop(other, "fsdp", 2, 4, -1)
    early = [swap(left), swap(right), swap(other)]
    far_a, far_b, early = lax.optimization_barrier((far_a, far_b, early))
    other_far = [across(far_a), across(far_b)]
    near = [slab, left, right, other, far_a, far_b, other_left, other_right] + other_far
    late = [swap(piece) for piece in near[4:]]
    return near + [slab_swap] + early + late, norm


def places():
    me = lax.axis_index("fsdp")
    y, x, core = me // 8, (me // 2) % 4, me % 2
    steps = ((0, 0), (0, 3), (0, 1), (1, 0), (0, 2), (1, 3), (1, 1), (1, 2))
    found = []
    for c in (core, 1 - core):
        for i, o in steps:
            found.append(jnp.where(i == 0, y, 1 - y) * 8 + ((x + o) % 4) * 2 + c)
    found += [lax.axis_index("section"), core]
    return jnp.stack(found).astype(jnp.int32)


def gather_section(block):
    return lax.all_to_all(
        jnp.broadcast_to(block[None], (16,) + block.shape), "section", 0, 0, tiled=True
    )


def along_y(block):
    mate = hop(block, "section", 1, 2, 1)
    even = lax.axis_index("section") % 2 == 0
    return jnp.stack([jnp.where(even, block, mate), jnp.where(even, mate, block)])


def along_z(pair):
    planes = [list(range(y, 16, 2)) for y in range(2)]
    whole = lax.all_gather(pair, "section", axis=0, axis_index_groups=planes)
    return whole.reshape((16,) + pair.shape[1:])


def add(keep, got):
    return (keep.astype(F32) + got.astype(F32)).astype(BF16)


def among_chips(chunks):
    chips = [list(range(core, 16, 2)) for core in range(2)]
    return lax.all_to_all(chunks, "fsdp", 0, 0, tiled=True, axis_index_groups=chips)


def project(place_ref, x_ref, y_ref, *rest):
    pieces = rest[:16]
    out_ref, w_ref, xv_ref, yv_ref, sem = rest[16:]
    size, rank = pieces[0].shape[0], pieces[0].shape[1] // 2
    copies = [pltpu.make_async_copy(x_ref, xv_ref, sem.at[16])]
    for at, piece in enumerate(pieces):
        span = pl.ds(pl.multiple_of(place_ref[at] * size, size), size)
        copies.append(pltpu.make_async_copy(piece, w_ref.at[span, :], sem.at[at]))
    last = pltpu.make_async_copy(y_ref, yv_ref, sem.at[17])
    for copy in copies + [last]:
        copy.start()
    for copy in copies:
        copy.wait()
    out_ref[:, : 2 * rank] = dot(xv_ref[...], w_ref[...], NN).astype(BF16)
    last.wait()
    out_ref[:, 2 * rank :] = dot(yv_ref[...], w_ref[:, rank:], NN).astype(BF16)


def chain(width, s_ref, place_ref, a_hbm, norm_ref, x_hbm, y_hbm, *rest):
    pieces = rest[:20]
    keep_ref, send_ref, keep_part, send_part = rest[20:24]
    z_ref, a_ref, w_ref, lift_ref, act_ref, slope_ref, inv_ref = rest[24:31]
    q_ref, p_ref, sq_ref, x_ref, y_ref, sem = rest[31:]
    layers = a_ref.shape[0]
    rank = z_ref.shape[2]
    cut = [slice(rank * i, rank * (i + 1)) for i in range(layers)]
    parts, many = 4, layers // 4
    first = pltpu.make_async_copy(a_hbm, a_ref, sem.at[parts, 0])
    first.start()
    copies = []
    for part in range(parts):
        some = pl.ds(part * many, many)
        for at, whole in enumerate((0, 1, 2, 3, None, 6, 7, None) * 2):
            first_of = 10 * (at // 8)
            if whole is not None:
                piece = pieces[first_of + whole].at[some]
            else:
                half = first_of + (4 if at % 8 == 4 else 8) + part // 2
                piece = pieces[half].at[pl.ds(part % 2 * many, many)]
            span = pl.ds(pl.multiple_of(place_ref[at] * rank, rank), rank)
            copy = pltpu.make_async_copy(piece, z_ref.at[some, span, :], sem.at[part, at])
            copy.start()
            copies.append(copy)
    whole = [
        pltpu.make_async_copy(x_hbm, x_ref, sem.at[parts, 1]),
        pltpu.make_async_copy(y_hbm, y_ref, sem.at[parts, 2]),
    ]
    for copy in whole:
        copy.start()
    first.wait()
    for s in range(layers):
        w_ref[s] = a_ref[s, :, cut[1]].astype(F32)
        lift_ref[s] = a_ref[s, :, cut[2]].astype(F32)
    scale = 1.0 / width
    total = norm_ref[...]
    for s in range(layers):
        if s % many == 0:
            for copy in copies[16 * (s // many) : 16 * (s // many) + 16]:
                copy.wait()
        inverse = lax.rsqrt(jnp.maximum(total, 0.0) * scale + 1e-05)
        raw = a_ref[s, :, cut[0]].astype(F32)
        if s > 0:
            raw = raw + dot(q_ref[:, : rank * s], z_ref[s, : rank * s, :], NN)
        act = raw * inverse
        sigma = jax.nn.sigmoid(act)
        now = (act * sigma).astype(BF16)
        q_ref[:, cut[s]] = now
        slope_ref[s] = sigma * (1.0 + act * (1.0 - sigma))
        act_ref[s] = act
        inv_ref[s] = jnp.broadcast_to(inverse, act.shape)
        wide = now.astype(F32)
        ahead = dot(now, z_ref[s, rank * s :, :], NT)
        own = ahead[:, :rank]
        here = w_ref[s]
        total = total + jnp.sum(wide * (2.0 * here + own), axis=1, keepdims=True)
        w_ref[s] = here + own
        for k in range(s + 1, layers):
            w_ref[k] += ahead[:, cut[k - s]]
    shrink = jnp.zeros_like(total)
    for s in range(layers - 1, -1, -1):
        up = lift_ref[s]
        if s + 1 < layers:
            up = up - shrink * w_ref[s]
            up = up - dot(sq_ref[:, rank * (s + 1) :], z_ref[s, rank * (s + 1) :, :], NN)
        grad = (up * slope_ref[s]).astype(BF16).astype(F32)
        inverse = inv_ref[s]
        now = (grad * inverse).astype(BF16)
        p_ref[:, cut[s]] = now
        sq_ref[:, cut[s]] = (shrink * q_ref[:, cut[s]].astype(F32)).astype(BF16)
        if s > 0:
            back = dot(now, z_ref[s, : rank * s, :], NT)
            for k in range(s):
                lift_ref[k] += back[:, cut[k]]
        mean = jnp.sum(grad * act_ref[s] * inverse * inverse, axis=1, keepdims=True) * scale
        shrink = shrink + mean
    here = pl.ds(pl.multiple_of(s_ref[16] * rank, rank), rank)
    p_t, q_t, sq_t = p_ref[:, here].T, q_ref[:, here].T, sq_ref[:, here].T
    both = jnp.concatenate([p_t, -sq_t], axis=0)
    even_core = s_ref[17] == 0
    for i in range(layers // 2):
        span = slice(2 * rank * i, 2 * rank * (i + 1))
        before = dot(both, q_ref[:, span], NN)
        after = dot(q_t, p_ref[:, span], NN)
        scaled = -dot(q_t, sq_ref[:, span], NN)
        found = []
        for k in range(2):
            j, some = 2 * i + k, slice(rank * k, rank * (k + 1))
            later = jnp.where(j == s_ref[16], 0.0, after[:, some])
            later = jnp.concatenate([later, scaled[:, some]], axis=0)
            found.append(jnp.where(j < s_ref[16], before[:, some], later).astype(BF16))
        keep_ref[i] = jnp.where(even_core, found[0], found[1])
        send_ref[i] = jnp.where(even_core, found[1], found[0])

    for copy in whole:
        copy.wait()
    half, _, piece = keep_part.shape
    for i in range(half):
        span = slice(2 * piece * i, 2 * piece * (i + 1))
        from_x = dot(both, x_ref[:, span], NN)
        from_y = dot(q_t, y_ref[:, span], NN)
        sums = jnp.concatenate([from_x[:rank], from_x[rank:] + from_y], axis=0).astype(BF16)
        even, odd = sums[:, :piece], sums[:, piece:]
        keep_part[i] = jnp.where(even_core, even, odd)
        send_part[i] = jnp.where(even_core, odd, even)


def chain_call(place, projected, norm, x, y, table):
    sections, tokens, wide = projected.shape
    rank, width, piece = wide // 3, x.shape[1], x.shape[1] // 16
    smem = pl.BlockSpec(memory_space=pltpu.SMEM)
    vmem = pl.BlockSpec(memory_space=pltpu.VMEM)
    in_hbm = pl.BlockSpec(memory_space=pltpu.HBM)
    big = pltpu.VMEM((sections, tokens, rank), F32)
    flat = pltpu.VMEM((tokens, sections * rank), BF16)
    return pl.pallas_call(
        functools.partial(chain, width),
        out_shape=(
            jax.ShapeDtypeStruct((8, 2 * rank, rank), BF16),
            jax.ShapeDtypeStruct((8, 2 * rank, rank), BF16),
            jax.ShapeDtypeStruct((8, 2 * rank, piece), BF16),
            jax.ShapeDtypeStruct((8, 2 * rank, piece), BF16),
        ),
        in_specs=[smem, smem, in_hbm, vmem] + [in_hbm] * 22,
        out_specs=(vmem,) * 4,
        scratch_shapes=[pltpu.VMEM((sections, sections * rank, rank), BF16)]
        + [pltpu.VMEM((sections, tokens, wide), BF16)]
        + [big] * 5
        + [flat] * 3
        + [pltpu.VMEM(x.shape, BF16)] * 2
        + [pltpu.SemaphoreType.DMA((5, 16))],
        compiler_params=pltpu.CompilerParams(vmem_limit_bytes=57 * MIB),
        cost_estimate=pl.CostEstimate(
            flops=2 * 10**10, bytes_accessed=12 * MIB, transcendentals=10**6
        ),
        name="chain",
    )(place, place, projected, norm, x, y, *table)


def finish(s_ref, part_ref, mate_ref, up_hbm, down_hbm, own_ref, gain_ref, *rest):
    down_out, gain_out, up_out, up_ref, down_ref, sem = rest
    copies = [
        pltpu.make_async_copy(up_hbm, up_ref, sem.at[0]),
        pltpu.make_async_copy(down_hbm, down_ref, sem.at[1]),
    ]
    for copy in copies:
        copy.start()
    layers, rank, piece = up_ref.shape
    held = part_ref[0, :, :piece].astype(F32)
    for k in range(1, part_ref.shape[0]):
        held = held + part_ref[k, :, :piece].astype(F32)
    first = s_ref[17] == 0
    zero = jnp.zeros((rank, rank), BF16)
    masked, after = [], []
    for j in range(layers):
        ours, theirs = part_ref[j // 2, :, piece:], mate_ref[j // 2]
        sums = jnp.where(first == (j % 2 == 0), ours, theirs)
        before = jnp.where(j < s_ref[16], sums[:rank], zero)
        masked.append(jnp.concatenate([before, sums[rank:]], axis=0))
        after.append(jnp.where(j > s_ref[16], sums[:rank], zero))
    for copy in copies:
        copy.wait()
    held = held + dot(jnp.concatenate(masked, axis=1), up_ref[...].reshape(-1, piece), NN)
    held_up = held[rank:]
    for k in range(layers):
        held_up = held_up + dot(after[k], down_ref[k], NT)
    up_out[...] = held_up
    held_down = held[:rank]
    down_out[...] = (held_down * gain_ref[...].astype(F32)).T
    gain_out[...] = jnp.sum(own_ref[...].astype(F32).T * held_down, axis=0, keepdims=True)


def on_device(inputs, out_grad, down_proj, gain, up_proj):
    sections, groups = lax.axis_size("section"), lax.axis_size("fsdp")
    s = lax.axis_index("section")
    place = places()
    width = inputs.shape[2]
    x = inputs.reshape(-1, width)
    y = out_grad.reshape(-1, width)
    tokens = x.shape[0]
    down, gain_row, up = down_proj[0], gain[0].astype(F32), up_proj[0]
    piece, rank = down.shape
    smem = pl.BlockSpec(memory_space=pltpu.SMEM)
    vmem = pl.BlockSpec(memory_space=pltpu.VMEM)
    in_hbm = pl.BlockSpec(memory_space=pltpu.HBM)

    scaled_down = (down.astype(F32) * gain_row[:, None]).astype(BF16)
    weights = jnp.concatenate([scaled_down, up.T], axis=1)

    up_all = along_z(along_y(up))

    projected = pl.pallas_call(
        project,
        out_shape=jax.ShapeDtypeStruct((tokens, 3 * rank), BF16),
        in_specs=[smem] + [in_hbm] * 18,
        out_specs=vmem,
        scratch_shapes=[
            pltpu.VMEM((width, 2 * rank), BF16),
            pltpu.VMEM(x.shape, BF16),
            pltpu.VMEM(y.shape, BF16),
            pltpu.SemaphoreType.DMA((18,)),
        ],
        compiler_params=pltpu.CompilerParams(vmem_limit_bytes=57 * MIB),
        cost_estimate=pl.CostEstimate(
            flops=8 * 10**9, bytes_accessed=9 * MIB, transcendentals=0
        ),
        name="project",
    )(place, x, y, *gather_pieces(weights))
    up_all, pair, late = lax.optimization_barrier(
        (up_all, along_y(projected), along_y(scaled_down))
    )
    projected = along_z(pair)
    norm = jnp.sum(jnp.square(x.astype(F32)), axis=1, keepdims=True)

    pairs = dot(up_all.reshape(sections * rank, piece), weights, NN)
    layer = lax.broadcasted_iota(jnp.int32, (sections * rank, 1), 0) // rank
    chosen = jnp.where(layer < s, pairs[:, :rank], pairs[:, rank:]).astype(BF16)
    chosen = chosen.reshape(groups, rank, rank)
    chosen = lax.all_to_all(chosen, "fsdp", 0, 0, tiled=True)
    block = jnp.sum(chosen.astype(F32), axis=0).astype(BF16)
    block, late = lax.optimization_barrier((block, late))
    table, norm = gather_table(gather_section(block), norm)
    down_all = along_z(late)

    cross, cross_out, part, part_out = chain_call(place, projected, norm, x, y, table)
    cross_got, part_out = lax.optimization_barrier((swap(cross_out), part_out))
    cross = among_chips(add(cross, cross_got))
    part_got = swap(part_out)
    cross = jnp.sum(cross.astype(F32), axis=0).astype(BF16)
    half = groups // 2
    cross = jnp.broadcast_to(cross[None], (half, 2 * rank, rank))
    part = among_chips(jnp.concatenate([add(part, part_got), cross], axis=2))
    mate = swap(part[:, :, piece:])

    grad_down, grad_gain, grad_up = pl.pallas_call(
        finish,
        out_shape=(
            jax.ShapeDtypeStruct((piece, rank), F32),
            jax.ShapeDtypeStruct((1, piece), F32),
            jax.ShapeDtypeStruct((rank, piece), F32),
        ),
        in_specs=[smem, vmem, vmem, in_hbm, in_hbm, vmem, vmem],
        out_specs=(vmem,) * 3,
        scratch_shapes=[
            pltpu.VMEM(up_all.shape, BF16),
            pltpu.VMEM(down_all.shape, BF16),
            pltpu.SemaphoreType.DMA((2,)),
        ],
        compiler_params=pltpu.CompilerParams(vmem_limit_bytes=57 * MIB),
        name="finish",
    )(place, part, mate, up_all, down_all, down, gain)
    return (grad_down[None], grad_gain, grad_up[None])


def solution(mesh):
    placed = (
        P(None, "fsdp", None),
        P(None, "fsdp", None),
        P("section", "fsdp", None),
        P("section", "fsdp"),
        P("section", None, "fsdp"),
    )
    return jax.shard_map(
        on_device,
        mesh=mesh,
        in_specs=placed,
        out_specs=(P("section", "fsdp", None), P("section", "fsdp"), P("section", None, "fsdp")),
        check_vma=False,
    )
```

```python
import functools

import jax
import jax.numpy as jnp
from jax import lax
from jax.experimental import pallas as pl
from jax.experimental.pallas import tpu as pltpu
from jax.sharding import PartitionSpec as P

F32 = jnp.float32
BF16 = jnp.bfloat16
NN = ((1,), (0,))
NT = ((1,), (1,))
TN = ((0,), (0,))
MIB = 2**20


def dot(a, b, dims):
    return lax.dot_general(a, b, (dims, ((), ())), preferred_element_type=F32)


def hop(block, axis, stride, count, offset):
    route = []
    for i in range(lax.axis_size(axis)):
        place = (i // stride) % count
        route.append((i, i + ((place + offset) % count - place) * stride))
    return lax.ppermute(block, axis, route)


def swap(block):
    return hop(block, "fsdp", 1, 2, 1)


def across(block):
    route = []
    for section in range(16):
        for group in range(16):
            to = (section ^ 1) * 16 + (group ^ 8)
            route.append((section * 16 + group, to))
    return lax.ppermute(block, ("section", "fsdp"), route)


def gather_pieces(shard):
    left = hop(shard, "fsdp", 2, 4, 1)
    right = hop(shard, "fsdp", 2, 4, -1)
    other = hop(shard, "fsdp", 8, 2, 1)
    far = hop(left, "fsdp", 2, 4, 1)
    other_left = hop(other, "fsdp", 2, 4, 1)
    other_right = hop(other, "fsdp", 2, 4, -1)
    other_far = hop(other_right, "fsdp", 2, 4, -1)
    near = [shard, left, right, other, far, other_left, other_right, other_far]
    return near + [swap(piece) for piece in near]


def gather_table(slab):
    half = slab.shape[0] // 2
    slab_swap = swap(slab)
    left = hop(slab, "fsdp", 2, 4, 1)
    right = hop(slab, "fsdp", 2, 4, -1)
    other = across(slab)
    far_a = hop(left[:half], "fsdp", 2, 4, 1)
    far_b = hop(right[half:], "fsdp", 2, 4, -1)
    other, slab_swap = lax.optimization_barrier((other, slab_swap))
    other_left = hop(other, "fsdp", 2, 4, 1)
    other_right = hop(other, "fsdp", 2, 4, -1)
    early = [swap(left), swap(right), swap(other)]
    far_a, far_b, early = lax.optimization_barrier((far_a, far_b, early))
    other_far = [across(far_a), across(far_b)]
    near = [slab, left, right, other, far_a, far_b, other_left, other_right] + other_far
    late = [swap(piece) for piece in near[4:]]
    return near + [slab_swap] + early + late


def places():
    me = lax.axis_index("fsdp")
    y, x, core = me // 8, (me // 2) % 4, me % 2
    steps = ((0, 0), (0, 3), (0, 1), (1, 0), (0, 2), (1, 3), (1, 1), (1, 2))
    found = []
    for c in (core, 1 - core):
        for i, o in steps:
            found.append(jnp.where(i == 0, y, 1 - y) * 8 + ((x + o) % 4) * 2 + c)
    found += [lax.axis_index("section"), core]
    return jnp.stack(found).astype(jnp.int32)


def gather_section(block):
    return lax.all_to_all(
        jnp.broadcast_to(block[None], (16,) + block.shape), "section", 0, 0, tiled=True
    )


def along_y(block):
    mate = hop(block, "section", 1, 2, 1)
    even = lax.axis_index("section") % 2 == 0
    return jnp.stack([jnp.where(even, block, mate), jnp.where(even, mate, block)])


def along_z(pair):
    planes = [list(range(y, 16, 2)) for y in range(2)]
    whole = lax.all_gather(pair, "section", axis=0, axis_index_groups=planes)
    return whole.reshape((16,) + pair.shape[1:])


def add(keep, got):
    return (keep.astype(F32) + got.astype(F32)).astype(BF16)


def among_chips(chunks):
    chips = [list(range(core, 16, 2)) for core in range(2)]
    return lax.all_to_all(chunks, "fsdp", 0, 0, tiled=True, axis_index_groups=chips)


def project(place_ref, x_ref, y_ref, *rest):
    pieces = rest[:16]
    out_ref, w_ref, xv_ref, yv_ref, sem = rest[16:]
    size, rank = pieces[0].shape[0], pieces[0].shape[1] // 2
    copies = [pltpu.make_async_copy(x_ref, xv_ref, sem.at[16])]
    for at, piece in enumerate(pieces):
        span = pl.ds(pl.multiple_of(place_ref[at] * size, size), size)
        copies.append(pltpu.make_async_copy(piece, w_ref.at[span, :], sem.at[at]))
    last = pltpu.make_async_copy(y_ref, yv_ref, sem.at[17])
    for copy in copies + [last]:
        copy.start()
    for copy in copies:
        copy.wait()
    out_ref[:, : 2 * rank] = dot(xv_ref[...], w_ref[...], NN).astype(BF16)
    last.wait()
    out_ref[:, 2 * rank :] = dot(yv_ref[...], w_ref[:, rank:], NN).astype(BF16)


def chain(width, s_ref, place_ref, a_hbm, norm_ref, x_hbm, y_hbm, *rest):
    pieces = rest[:20]
    keep_ref, send_ref, keep_part, send_part = rest[20:24]
    z_ref, a_ref, w_ref, lift_ref, act_ref, slope_ref, inv_ref = rest[24:31]
    q_ref, p_ref, sq_ref, x_ref, y_ref, sem = rest[31:]
    layers = a_ref.shape[0]
    rank = z_ref.shape[2]
    cut = [slice(rank * i, rank * (i + 1)) for i in range(layers)]
    parts, many = 4, layers // 4
    first = pltpu.make_async_copy(a_hbm, a_ref, sem.at[parts, 0])
    first.start()
    copies = []
    for part in range(parts):
        some = pl.ds(part * many, many)
        for at, whole in enumerate((0, 1, 2, 3, None, 6, 7, None) * 2):
            first_of = 10 * (at // 8)
            if whole is not None:
                piece = pieces[first_of + whole].at[some]
            else:
                half = first_of + (4 if at % 8 == 4 else 8) + part // 2
                piece = pieces[half].at[pl.ds(part % 2 * many, many)]
            span = pl.ds(pl.multiple_of(place_ref[at] * rank, rank), rank)
            copy = pltpu.make_async_copy(piece, z_ref.at[some, span, :], sem.at[part, at])
            copy.start()
            copies.append(copy)
    whole = [
        pltpu.make_async_copy(x_hbm, x_ref, sem.at[parts, 1]),
        pltpu.make_async_copy(y_hbm, y_ref, sem.at[parts, 2]),
    ]
    for copy in whole:
        copy.start()
    first.wait()
    for s in range(layers):
        w_ref[s] = a_ref[s, :, cut[1]].astype(F32)
        lift_ref[s] = a_ref[s, :, cut[2]].astype(F32)
    scale = 1.0 / width
    total = norm_ref[...]
    for s in range(layers):
        if s % many == 0:
            for copy in copies[16 * (s // many) : 16 * (s // many) + 16]:
                copy.wait()
        inverse = lax.rsqrt(jnp.maximum(total, 0.0) * scale + 1e-05)
        raw = a_ref[s, :, cut[0]].astype(F32)
        if s > 0:
            raw = raw + dot(q_ref[:, : rank * s], z_ref[s, : rank * s, :], NN)
        act = raw * inverse
        sigma = jax.nn.sigmoid(act)
        now = (act * sigma).astype(BF16)
        q_ref[:, cut[s]] = now
        slope_ref[s] = sigma * (1.0 + act * (1.0 - sigma))
        act_ref[s] = act
        inv_ref[s] = jnp.broadcast_to(inverse, act.shape)
        wide = now.astype(F32)
        ahead = dot(now, z_ref[s, rank * s :, :], NT)
        own = ahead[:, :rank]
        here = w_ref[s]
        total = total + jnp.sum(wide * (2.0 * here + own), axis=1, keepdims=True)
        w_ref[s] = here + own
        for k in range(s + 1, layers):
            w_ref[k] += ahead[:, cut[k - s]]
    shrink = jnp.zeros_like(total)
    for s in range(layers - 1, -1, -1):
        up = lift_ref[s]
        if s + 1 < layers:
            up = up - shrink * w_ref[s]
            up = up - dot(sq_ref[:, rank * (s + 1) :], z_ref[s, rank * (s + 1) :, :], NN)
        grad = (up * slope_ref[s]).astype(BF16).astype(F32)
        inverse = inv_ref[s]
        now = (grad * inverse).astype(BF16)
        p_ref[:, cut[s]] = now
        sq_ref[:, cut[s]] = (shrink * q_ref[:, cut[s]].astype(F32)).astype(BF16)
        if s > 0:
            back = dot(now, z_ref[s, : rank * s, :], NT)
            for k in range(s):
                lift_ref[k] += back[:, cut[k]]
        mean = jnp.sum(grad * act_ref[s] * inverse * inverse, axis=1, keepdims=True) * scale
        shrink = shrink + mean
    here = pl.ds(pl.multiple_of(s_ref[16] * rank, rank), rank)
    p_t, q_t, sq_t = p_ref[:, here].T, q_ref[:, here].T, sq_ref[:, here].T
    both = jnp.concatenate([p_t, -sq_t], axis=0)
    even_core = s_ref[17] == 0
    for i in range(layers // 2):
        span = slice(2 * rank * i, 2 * rank * (i + 1))
        before = dot(both, q_ref[:, span], NN)
        after = dot(q_t, p_ref[:, span], NN)
        scaled = -dot(q_t, sq_ref[:, span], NN)
        found = []
        for k in range(2):
            j, some = 2 * i + k, slice(rank * k, rank * (k + 1))
            later = jnp.where(j == s_ref[16], 0.0, after[:, some])
            later = jnp.concatenate([later, scaled[:, some]], axis=0)
            found.append(jnp.where(j < s_ref[16], before[:, some], later).astype(BF16))
        keep_ref[i] = jnp.where(even_core, found[0], found[1])
        send_ref[i] = jnp.where(even_core, found[1], found[0])

    for copy in whole:
        copy.wait()
    half, _, piece = keep_part.shape
    for i in range(half):
        span = slice(2 * piece * i, 2 * piece * (i + 1))
        from_x = dot(both, x_ref[:, span], NN)
        from_y = dot(q_t, y_ref[:, span], NN)
        sums = jnp.concatenate([from_x[:rank], from_x[rank:] + from_y], axis=0).astype(BF16)
        even, odd = sums[:, :piece], sums[:, piece:]
        keep_part[i] = jnp.where(even_core, even, odd)
        send_part[i] = jnp.where(even_core, odd, even)


def chain_call(place, projected, norm, x, y, table):
    sections, tokens, wide = projected.shape
    rank, width, piece = wide // 3, x.shape[1], x.shape[1] // 16
    smem = pl.BlockSpec(memory_space=pltpu.SMEM)
    vmem = pl.BlockSpec(memory_space=pltpu.VMEM)
    in_hbm = pl.BlockSpec(memory_space=pltpu.HBM)
    big = pltpu.VMEM((sections, tokens, rank), F32)
    flat = pltpu.VMEM((tokens, sections * rank), BF16)
    return pl.pallas_call(
        functools.partial(chain, width),
        out_shape=(
            jax.ShapeDtypeStruct((8, 2 * rank, rank), BF16),
            jax.ShapeDtypeStruct((8, 2 * rank, rank), BF16),
            jax.ShapeDtypeStruct((8, 2 * rank, piece), BF16),
            jax.ShapeDtypeStruct((8, 2 * rank, piece), BF16),
        ),
        in_specs=[smem, smem, in_hbm, vmem] + [in_hbm] * 22,
        out_specs=(vmem,) * 4,
        scratch_shapes=[pltpu.VMEM((sections, sections * rank, rank), BF16)]
        + [pltpu.VMEM((sections, tokens, wide), BF16)]
        + [big] * 5
        + [flat] * 3
        + [pltpu.VMEM(x.shape, BF16)] * 2
        + [pltpu.SemaphoreType.DMA((5, 16))],
        compiler_params=pltpu.CompilerParams(vmem_limit_bytes=57 * MIB),
        cost_estimate=pl.CostEstimate(
            flops=2 * 10**10, bytes_accessed=12 * MIB, transcendentals=10**6
        ),
        name="chain",
    )(place, place, projected, norm, x, y, *table)


def finish(s_ref, part_ref, mate_ref, up_hbm, down_hbm, own_ref, gain_ref, *rest):
    down_out, gain_out, up_out, up_ref, down_ref, sem = rest
    copies = [
        pltpu.make_async_copy(up_hbm, up_ref, sem.at[0]),
        pltpu.make_async_copy(down_hbm, down_ref, sem.at[1]),
    ]
    for copy in copies:
        copy.start()
    layers, rank, piece = up_ref.shape
    held = part_ref[0, :, :piece].astype(F32)
    for k in range(1, part_ref.shape[0]):
        held = held + part_ref[k, :, :piece].astype(F32)
    first = s_ref[17] == 0
    zero = jnp.zeros((rank, rank), BF16)
    masked, after = [], []
    for j in range(layers):
        ours, theirs = part_ref[j // 2, :, piece:], mate_ref[j // 2]
        sums = jnp.where(first == (j % 2 == 0), ours, theirs)
        before = jnp.where(j < s_ref[16], sums[:rank], zero)
        masked.append(jnp.concatenate([before, sums[rank:]], axis=0))
        after.append(jnp.where(j > s_ref[16], sums[:rank], zero))
    for copy in copies:
        copy.wait()
    held = held + dot(jnp.concatenate(masked, axis=1), up_ref[...].reshape(-1, piece), NN)
    held_up = held[rank:]
    for k in range(layers):
        held_up = held_up + dot(after[k], down_ref[k], NT)
    up_out[...] = held_up
    held_down = held[:rank]
    down_out[...] = (held_down * gain_ref[...].astype(F32)).T
    gain_out[...] = jnp.sum(own_ref[...].astype(F32).T * held_down, axis=0, keepdims=True)


def on_device(inputs, out_grad, down_proj, gain, up_proj):
    sections, groups = lax.axis_size("section"), lax.axis_size("fsdp")
    s = lax.axis_index("section")
    place = places()
    width = inputs.shape[2]
    x = inputs.reshape(-1, width)
    y = out_grad.reshape(-1, width)
    tokens = x.shape[0]
    down, gain_row, up = down_proj[0], gain[0].astype(F32), up_proj[0]
    piece, rank = down.shape
    smem = pl.BlockSpec(memory_space=pltpu.SMEM)
    vmem = pl.BlockSpec(memory_space=pltpu.VMEM)
    in_hbm = pl.BlockSpec(memory_space=pltpu.HBM)

    scaled_down = (down.astype(F32) * gain_row[:, None]).astype(BF16)
    weights = jnp.concatenate([scaled_down, up.T], axis=1)

    up_all = along_z(along_y(up))

    projected = pl.pallas_call(
        project,
        out_shape=jax.ShapeDtypeStruct((tokens, 3 * rank), BF16),
        in_specs=[smem] + [in_hbm] * 18,
        out_specs=vmem,
        scratch_shapes=[
            pltpu.VMEM((width, 2 * rank), BF16),
            pltpu.VMEM(x.shape, BF16),
            pltpu.VMEM(y.shape, BF16),
            pltpu.SemaphoreType.DMA((18,)),
        ],
        compiler_params=pltpu.CompilerParams(vmem_limit_bytes=57 * MIB),
        cost_estimate=pl.CostEstimate(
            flops=8 * 10**9, bytes_accessed=9 * MIB, transcendentals=0
        ),
        name="project",
    )(place, x, y, *gather_pieces(weights))
    up_all, pair, late = lax.optimization_barrier(
        (up_all, along_y(projected), along_y(scaled_down))
    )
    projected = along_z(pair)
    norm = jnp.sum(jnp.square(x.astype(F32)), axis=1, keepdims=True)

    pairs = dot(up_all.reshape(sections * rank, piece), weights, NN)
    layer = lax.broadcasted_iota(jnp.int32, (sections * rank, 1), 0) // rank
    chosen = jnp.where(layer < s, pairs[:, :rank], pairs[:, rank:]).astype(BF16)
    chosen = chosen.reshape(groups, rank, rank)
    chosen = lax.all_to_all(chosen, "fsdp", 0, 0, tiled=True)
    block = jnp.sum(chosen.astype(F32), axis=0).astype(BF16)
    block, late = lax.optimization_barrier((block, late))
    table = gather_table(gather_section(block))
    down_all = along_z(late)

    cross, cross_out, part, part_out = chain_call(place, projected, norm, x, y, table)
    cross_got, part_out = lax.optimization_barrier((swap(cross_out), part_out))
    cross = among_chips(add(cross, cross_got))
    part_got = swap(part_out)
    cross = jnp.sum(cross.astype(F32), axis=0).astype(BF16)
    half = groups // 2
    cross = jnp.broadcast_to(cross[None], (half, 2 * rank, rank))
    part = among_chips(jnp.concatenate([add(part, part_got), cross], axis=2))
    mate = swap(part[:, :, piece:])

    grad_down, grad_gain, grad_up = pl.pallas_call(
        finish,
        out_shape=(
            jax.ShapeDtypeStruct((piece, rank), F32),
            jax.ShapeDtypeStruct((1, piece), F32),
            jax.ShapeDtypeStruct((rank, piece), F32),
        ),
        in_specs=[smem, vmem, vmem, in_hbm, in_hbm, vmem, vmem],
        out_specs=(vmem,) * 3,
        scratch_shapes=[
            pltpu.VMEM(up_all.shape, BF16),
            pltpu.VMEM(down_all.shape, BF16),
            pltpu.SemaphoreType.DMA((2,)),
        ],
        compiler_params=pltpu.CompilerParams(vmem_limit_bytes=57 * MIB),
        name="finish",
    )(place, part, mate, up_all, down_all, down, gain)
    return (grad_down[None], grad_gain, grad_up[None])


def solution(mesh):
    placed = (
        P(None, "fsdp", None),
        P(None, "fsdp", None),
        P("section", "fsdp", None),
        P("section", "fsdp"),
        P("section", None, "fsdp"),
    )
    return jax.shard_map(
        on_device,
        mesh=mesh,
        in_specs=placed,
        out_specs=(P("section", "fsdp", None), P("section", "fsdp"), P("section", None, "fsdp")),
        check_vma=False,
    )
```
